256 devices in a mesh: front: 64 (over x, y, z_lo, core), blk: 4 (over z_hi).
Axes of the slice: x: 4, y: 4, z: 8 (z_hi: 4, z_lo: 2; z = z_hi * 2 + z_lo), core: 2. Of those that a mesh axis runs over, the one named last changes fastest.
Arguments:
- child_diag: float32 [65536, 1024], P(('front', 'blk')), as said below
- child_top: float32 [32768, 1024], P(('front', 'blk')), may hold values from -0.078125 to 0.078125
- child_rows: float32 [131072, 1024], P(('front', 'blk')), may hold values from -12 to 12
- row_owner: int32 [64, 16, 1], P('front'), may hold values from 0 to 63; in each aligned block of 16 rows (0 to 15, 16 to 31, ..., all dimensions but the last counted through in order) at most 2 rows name the same one
- row_slot: int32 [64, 16], P('front'), may hold values from 0 to 3
- col_block: int32 [64, 4], P('front'), may hold values from 0 to 1
- parent_diag: float32 [1024, 1024], P('blk'), as said below
- parent_rows: float32 [32768, 1024], P('front', 'blk'), may hold values from -6 to 6
Outputs:
- parent_factor: float32 [1024, 1024], P('blk')
- parent_panel: float32 [32768, 1024], P(('front', 'blk'))
The draws below stay inside these ranges and needn't reach their ends.
Inputs may be any that keep to these rules, and one draw needn't show every extreme that they name: `row_owner`: within the 16 row blocks of one child no owner is named more than 2 times, and in some children one owner is named exactly 2 times. `child_diag`: each 1024 x 1024 block is symmetric with all eigenvalues at least 1. `parent_diag`: symmetric with all eigenvalues at least 24; parent_diag - diag_update has all eigenvalues at least 12.
All inputs are finite; a program needn't handle non-finite values.
Results may differ from the reference program's by a relative error of at most 0.0001.
Values sent between devices are 32-bit elements; how exact they have to be, the bound alone decides.
A program may use at most 192 MiB of HBM per device.

```python
import math
import jax
import jax.numpy as jnp
import numpy as np
from jax import lax

W = 1024
TILE = 128
TA = 4
PB = 4
FRONTS = 64
BLOCKS = 4
CQ = 2
CAP = 2
TOP_ROWS = 32768
CHILD_ROWS = 131072
PARENT_ROWS = 32768
N_FRONT = 64
N_BLK = 4


def gram_blocks(samples, shift):
    product = jnp.einsum('aik,ajk->aij', samples, samples, precision=lax.Precision.HIGHEST) / W
    return product + shift * jnp.eye(W, dtype=jnp.float32)[None]


def draw_child_diag(key, part):
    subkey = jax.random.fold_in(key, 11)
    samples = jax.random.truncated_normal(subkey, -6.0, 6.0, (FRONTS, W, W), jnp.float32)
    return gram_blocks(samples, 1.0).reshape(FRONTS * W, W)


def draw_parent_diag(key, part):
    subkey = jax.random.fold_in(key, 23)
    samples = jax.random.truncated_normal(subkey, -6.0, 6.0, (1, W, W), jnp.float32)
    return gram_blocks(samples, 24.0).reshape(W, W)


def touch_ends(values, rng, low, top_value):
    shape = values.shape
    place = [jax.random.randint(jax.random.fold_in(rng, axis), (), 0, shape[axis]) for axis in range(len(shape))]
    values = values.at[tuple(place)].set(low)
    longest = shape.index(max(shape))
    place[longest] = (place[longest] + 1) % shape[longest]
    return values.at[tuple(place)].set(top_value)


def level_of(rng, extent, shards, smallest, largest):
    level, own = 1.0, jax.random.fold_in(rng, 6)
    for dim, parts in shards:
        steps = jnp.exp(jax.random.uniform(jax.random.fold_in(own, dim), (parts,), jnp.float32, smallest / len(shards), largest / len(shards)))
        level = level * jnp.repeat(steps, extent[dim] // parts).reshape([-1 if axis == dim else 1 for axis in range(len(extent))])
    return level


def shared_out(own_key, own, number, rows, number_of, top, most, skew):
    order = jax.random.permutation(own_key, number_of)
    heavy_load, usual = shares(number_of, rows * top, most, skew, True), shares(number_of, rows * top, most, skew, False)
    places = jnp.arange(number_of)

    def named(lengths, turn):
        used = int((lengths > 0).sum())
        fixed = max(1, used // 4)
        moved = fixed + (places - fixed + turn * (used - fixed)) % max(1, number_of - fixed)
        return jnp.zeros((number_of,), jnp.int32).at[order[jnp.where(places < fixed, places, moved)]].set(jnp.asarray(lengths, jnp.int32))

    lengths = jnp.where(number % 4 == 0, named(heavy_load, number // 4), named(usual, number - number // 4 - 1))
    mixed = jax.random.permutation(jax.random.fold_in(own, 3), number_of)
    giver, taker = mixed[0:number_of // 2 * 2:2], mixed[1:number_of // 2 * 2:2]
    margin = jnp.minimum(lengths[giver] - 1, most - lengths[taker]) // 2
    margin = jnp.where((giver == order[0]) | (taker == order[0]) | (lengths[taker] == 0), 0, jnp.maximum(margin, 0))
    moved = jax.random.randint(jax.random.fold_in(own, 4), (number_of // 2,), 0, 1 << 20) % (margin + 1)
    lengths = lengths.at[giver].add(-moved).at[taker].add(moved)
    members = jnp.searchsorted(jnp.cumsum(lengths), jnp.arange(rows * top), side="right").astype(jnp.int32)
    listing = members.reshape(top, rows).T
    listing = listing[jax.random.permutation(jax.random.fold_in(own, 1), rows)]
    turn = jax.random.randint(jax.random.fold_in(own, 2), (rows, 1), 0, top)
    return jnp.take_along_axis(listing, (jnp.arange(top)[None, :] + turn) % top, axis=1)


def shares(count, total, most, lean, full):
    weights = [(1 << 20) // math.isqrt(rank ** lean) + 1 for rank in range(1, count + 1)]
    largest = most if full else min(most, max(-(-total // count), total * weights[0] // sum(weights)))
    least = 1 if total - largest >= count - 1 else 0
    holding, surplus = [largest] + [least] * (count - 1), total - largest - least * (count - 1)
    while surplus > 0:
        movable = [i for i in range(1, count) if holding[i] < largest] or [i for i in range(1, count) if holding[i] < most]
        pool, left = sum([weights[i] for i in movable]), surplus
        for i in movable:
            addition = min(most - holding[i], max(1, left * weights[i] // pool), surplus)
            holding[i] = holding[i] + addition
            surplus = surplus - addition
    return np.array(holding)


def bell_draw(own_key, extent, width, most, shards=(), kind=jnp.bfloat16):
    entries = jax.random.normal(own_key, extent, jnp.float32) * width
    if len(shards) > 0:
        entries = level_of(own_key, extent, shards, -0.22, 0.18) * entries
    return jnp.clip(entries, min=-most, max=most).astype(kind)


def setup_inputs(seed: int = 0) -> dict:
    keys = jax.random.split(jax.random.key(seed), 9)
    child_diag = draw_child_diag(jax.random.fold_in(keys[8], 71), 0)
    child_top = bell_draw(keys[1], (TOP_ROWS, W), 0.0125, 0.078125, ((0, 256),), jnp.float32)
    child_rows = bell_draw(keys[2], (CHILD_ROWS, W), 2.0, 12.0, ((0, 256),), jnp.float32)
    row_owner_keys = jax.random.split(jax.random.fold_in(keys[3], 1), FRONTS * (BLOCKS * TA) // (BLOCKS * TA))
    row_owner_turns = jax.random.permutation(jax.random.fold_in(keys[3], 3), FRONTS * (BLOCKS * TA) // (BLOCKS * TA))
    row_owner = jax.vmap(lambda own, number: shared_out(jax.random.fold_in(keys[3], 2), own, number, BLOCKS * TA, FRONTS, 1, CAP, 2))(row_owner_keys, row_owner_turns).reshape((FRONTS, BLOCKS * TA, 1))
    row_slot = touch_ends(jax.random.randint(keys[4], (FRONTS, BLOCKS * TA), 0, PB), jax.random.fold_in(keys[4], 1), 0, PB - 1).astype(jnp.int32)
    col_block = touch_ends(jax.random.randint(keys[5], (FRONTS, BLOCKS), 0, CQ), jax.random.fold_in(keys[5], 1), 0, CQ - 1).astype(jnp.int32)
    parent_diag = draw_parent_diag(jax.random.fold_in(keys[8], 71), 0)
    parent_rows = bell_draw(keys[7], (PARENT_ROWS, W), 1.0, 6.0, ((0, 64), (1, 4)), jnp.float32)
    return dict(child_diag=child_diag, child_top=child_top, child_rows=child_rows, row_owner=row_owner, row_slot=row_slot, col_block=col_block, parent_diag=parent_diag, parent_rows=parent_rows)


HIGHEST = lax.Precision.HIGHEST

def right_solve(factor, matrix):
    return jax.scipy.linalg.solve_triangular(factor, matrix.T, lower=True).T

def reference(child_diag, child_top, child_rows, row_owner, row_slot, col_block, parent_diag, parent_rows):
    block_width = W // TILE
    diag_stack = child_diag.reshape(N_FRONT, W, W)
    top_stack = child_top.reshape(N_FRONT, N_BLK * TILE, W)
    rows_stack = child_rows.reshape(N_FRONT, N_BLK * TA * TILE, W)
    targets = (row_owner.reshape(N_FRONT, N_BLK * TA) * PB + row_slot).astype(jnp.int32)
    columns = (jnp.arange(N_BLK, dtype=jnp.int32)[None, :] * CQ + col_block).astype(jnp.int32)

    def one_child(carry, inputs):
        panel_update, diag_update = carry
        diag_block, top_block, rows_block, target_row, column_row = inputs
        factor = jnp.linalg.cholesky(diag_block)
        top_solved = right_solve(factor, top_block)
        rows_solved = right_solve(factor, rows_block)
        schur_tiles = jnp.dot(rows_solved, top_solved.T, precision=HIGHEST)
        schur_tiles = schur_tiles.reshape(N_BLK * TA, TILE, N_BLK, TILE).transpose(0, 2, 1, 3)
        panel_update = panel_update.at[target_row[:, None], :, column_row[None, :], :].add(schur_tiles)
        cross_terms = jnp.dot(top_solved, top_solved.T, precision=HIGHEST)
        cross_terms = cross_terms.reshape(N_BLK, TILE, N_BLK, TILE).transpose(0, 2, 1, 3)
        diag_update = diag_update.at[column_row[:, None], :, column_row[None, :], :].add(cross_terms)
        return ((panel_update, diag_update), None)
    panel_zero = jnp.zeros((N_FRONT * PB, TILE, block_width, TILE), jnp.float32)
    diag_zero = jnp.zeros((block_width, TILE, block_width, TILE), jnp.float32)
    (panel_update, diag_update), unused = lax.scan(one_child, (panel_zero, diag_zero), (diag_stack, top_stack, rows_stack, targets, columns))
    parent_factor = jnp.linalg.cholesky(parent_diag - diag_update.reshape(W, W))
    updated = parent_rows - panel_update.reshape(N_FRONT * PB * TILE, W)
    parent_panel = right_solve(parent_factor, updated)
    return (parent_factor, parent_panel)
```

```python
import functools
import jax
import jax.numpy as jnp
from jax import lax
from jax.experimental import pallas as pl
from jax.experimental.pallas import tpu as pltpu
from jax.sharding import PartitionSpec as P

W = 1024
TILE = 128
TA = 4
PB = 4
SUB = 8
HIGHEST=lax.Precision.HIGHEST
NT=(((1,),(1,)),((),()))

def dot_nt(a,b):
    return lax.dot_general(a,b,NT,precision=HIGHEST,preferred_element_type=jnp.float32)

def split(x):
    hi=x.astype(jnp.bfloat16)
    lo=(x-hi.astype(jnp.float32)).astype(jnp.bfloat16)
    return hi,lo

def dot3(ah,al,bh,bl):
    f=lambda p,q: lax.dot_general(p,q,NT,preferred_element_type=jnp.float32)
    return f(ah,bh)+(f(ah,bl)+f(al,bh))

def recip(x):
    r=pl.reciprocal(x,approx=True)
    r=r*(2.0-x*r)
    return r*(2.0-x*r)

def diag_steps(s):
    lane=lax.broadcasted_iota(jnp.int32,(SUB,TILE),1)
    sub=lax.broadcasted_iota(jnp.int32,(SUB,TILE),0)
    full=(SUB,TILE)
    for b in range(TILE//SUB):
        r0=b*SUB
        inside=(lane>=r0)&(lane<r0+SUB)
        v=[jnp.broadcast_to(s[r0+i:r0+i+1,:],full) for i in range(SUB)]
        a=[[jnp.broadcast_to(v[i][:,r0+j:r0+j+1],full) for j in range(i+1)] for i in range(SUB)]
        w=[jnp.where(inside,jnp.where(lane==r0+i,1.0,0.0),v[i]) for i in range(SUB)]
        r=[None]*SUB
        l=[[None]*SUB for _ in range(SUB)]
        for i in range(SUB):
            r[i]=recip(a[i][i])
            for k in range(i+1,SUB):
                l[k][i]=a[k][i]*r[i]
            for k in range(i+1,SUB):
                for m in range(i+1,k+1):
                    a[k][m]=a[k][m]-l[k][i]*a[m][i]
            for k in range(i+1,SUB):
                w[k]=w[k]-l[k][i]*w[i]
        z=[w[i]*r[i] for i in range(SUB)]
        for i in range(SUB-1,0,-1):
            for k in range(i):
                z[k]=z[k]-l[i][k]*z[i]
        for rb in range(b+1,TILE//SUB):
            x=s[rb*SUB:(rb+1)*SUB,:]
            c=[jnp.broadcast_to(x[:,r0+i:r0+i+1],full) for i in range(SUB)]
            p=c[0]*z[0]
            q=c[1]*z[1]
            for i in range(2,SUB,2):
                p=p+c[i]*z[i]
                q=q+c[i+1]*z[i+1]
            s[rb*SUB:(rb+1)*SUB,:]=jnp.where(inside,0.0,x)-(p+q)
        o=w[0]*lax.rsqrt(a[0][0])
        for i in range(1,SUB):
            o=jnp.where(sub==i,w[i]*lax.rsqrt(a[i][i]),o)
        s[r0:r0+SUB,:]=jnp.where(lane<r0+SUB,o,0.0)
        yield b

def diag(s):
    for _ in diag_steps(s): pass


def block(start,size=TILE):
    return pl.ds(pl.multiple_of(start,TILE),size)

def chol_solve(m,x,n,s,inv_hi,inv_lo,p_hi,p_lo,low=None,chunk=256):
    s[...]=m[0:TILE,0:TILE]
    if low is not None:
        low[...]=jnp.zeros((W,W),jnp.float32)
        low[0:TILE,0:TILE]=m[0:TILE,0:TILE]
    diag(s)
    rows=lax.broadcasted_iota(jnp.int32,(chunk,TILE),0)
    def step(j,carry):
        c0=j*TILE; c1=c0+TILE
        inv=s[...]
        ih,il=split(inv)
        inv_hi[...]=ih; inv_lo[...]=il
        if low is not None:
            low[block(c0),block(c0)]=dot_nt(low[block(c0),block(c0)],inv)
        p=dot_nt(m[block(c1),block(c0)],inv)
        new=m[block(c1),block(c1)]-dot_nt(p,p)
        s[...]=new
        if low is not None:
            low[block(c1),block(c1)]=new
        def panel(k):
            r=slice(k*chunk,(k+1)*chunk)
            a,b=split(m[r,block(c0)])
            q=dot3(a,b,inv_hi[...],inv_lo[...])
            q=jnp.where(rows+k*chunk>=c1,q,0.0)
            a,b=split(q)
            p_hi[r,:]=a; p_lo[r,:]=b
            if low is not None:
                low[r,block(c0)]=low[r,block(c0)]+q
        def trail(k):
            r=slice(k*chunk,(k+1)*chunk)
            m[r,:]=m[r,:]-dot3(p_hi[r,:],p_lo[r,:],p_hi[...],p_lo[...])
        def other(k,size):
            r=slice(k*size,(k+1)*size)
            a,b=split(x[r,block(c0)])
            q=dot3(a,b,inv_hi[...],inv_lo[...])
            a,b=split(q)
            x[r,:]=x[r,:]-dot3(a,b,p_hi[...],p_lo[...])
            x[r,block(c0)]=q
        size=min(chunk,n)
        work=[functools.partial(panel,k) for k in range(W//chunk)]
        work+=[functools.partial(trail,k) for k in range(W//chunk)]
        work+=[functools.partial(other,k,size) for k in range(n//size)]
        steps=TILE//SUB
        done=0
        for b in diag_steps(s):
            upto=(b+1)*len(work)//steps
            for f in work[done:upto]: f()
            done=upto
        return carry
    lax.fori_loop(0,W//TILE-1,step,0)
    c0=W-TILE
    inv=s[...]
    a,b=split(inv)
    inv_hi[...]=a; inv_lo[...]=b
    if low is not None:
        low[c0:,c0:]=dot_nt(low[c0:,c0:],inv)
    size=min(chunk,n)
    for k in range(n//size):
        r=slice(k*size,(k+1)*size)
        a,b=split(x[r,c0:])
        x[r,c0:]=dot3(a,b,inv_hi[...],inv_lo[...])

def scratch():
    b=jnp.bfloat16
    return [pltpu.VMEM((TILE,TILE),jnp.float32),pltpu.VMEM((TILE,TILE),b),pltpu.VMEM((TILE,TILE),b),
            pltpu.VMEM((W,TILE),b),pltpu.VMEM((W,TILE),b)]

HBM=pl.BlockSpec(memory_space=pl.ANY)
VM=pl.BlockSpec(memory_space=pltpu.VMEM)

def child_kernel(a_ref,top_ref,rows_ref,schur_ref,cross_ref,m,x,th,tl,sems,*rest):
    T=top_ref.shape[0]; n=T+rows_ref.shape[0]
    cp=[pltpu.make_async_copy(a_ref,m,sems.at[0]),pltpu.make_async_copy(top_ref,x.at[0:T],sems.at[1]),
        pltpu.make_async_copy(rows_ref,x.at[T:n],sems.at[2])]
    for c in cp: c.start()
    for c in cp: c.wait()
    chol_solve(m,x,n,*rest)
    for k in range(T//TILE):
        r=slice(k*TILE,(k+1)*TILE)
        a,b=split(x[r,:]); th[r,:]=a; tl[r,:]=b
    me=lax.axis_index("blk")
    cross_ref[...]=dot_nt(x[pl.ds(pl.multiple_of(me*TILE,TILE),TILE),:],x[0:T,:])
    for k in range((n-T)//TILE):
        r=slice(k*TILE,(k+1)*TILE)
        a,b=split(x[T+k*TILE:T+(k+1)*TILE,:])
        y=dot3(a,b,th[...],tl[...])
        for q in range(T//TILE):
            schur_ref[q,r,:]=y[:,q*TILE:(q+1)*TILE]

def child(a,top,rows):
    T=top.shape[0]; n=T+rows.shape[0]
    return pl.pallas_call(child_kernel,
        out_shape=(jax.ShapeDtypeStruct((T//TILE,rows.shape[0],TILE),jnp.float32),jax.ShapeDtypeStruct((TILE,T),jnp.float32)),
        in_specs=[HBM]*3,out_specs=(VM,VM),
        scratch_shapes=[pltpu.VMEM((W,W),jnp.float32),pltpu.VMEM((n,W),jnp.float32),
          pltpu.VMEM((T,W),jnp.bfloat16),pltpu.VMEM((T,W),jnp.bfloat16),pltpu.SemaphoreType.DMA((3,))]+scratch(),
        compiler_params=pltpu.CompilerParams(vmem_limit_bytes=56*2**20),name="child",
        cost_estimate=pl.CostEstimate(flops=6*2**30,bytes_accessed=2**24,transcendentals=0))(a,top,rows)

def parent_kernel(a_ref,low_ref,inv_ref,m,sem,*rest):
    c=pltpu.make_async_copy(a_ref,m,sem); c.start(); c.wait()
    inv_ref[...]=jnp.where(lax.broadcasted_iota(jnp.int32,(W,W),0)==lax.broadcasted_iota(jnp.int32,(W,W),1),1.0,0.0)
    chol_solve(m,inv_ref,W,*rest,low=low_ref)

def parent(a):
    return pl.pallas_call(parent_kernel,
        out_shape=(jax.ShapeDtypeStruct((W,W),jnp.float32),)*2,
        in_specs=[HBM],out_specs=(VM,VM),
        scratch_shapes=[pltpu.VMEM((W,W),jnp.float32),pltpu.SemaphoreType.DMA]+scratch(),
        compiler_params=pltpu.CompilerParams(vmem_limit_bytes=56*2**20),name="parent",
        cost_estimate=pl.CostEstimate(flops=6*2**30,bytes_accessed=2**24,transcendentals=0))(a)

def place_kernel(position,tiles,out,sems):
    copies=[pltpu.make_async_copy(tiles.at[i],out.at[position[i]],sems.at[i]) for i in range(tiles.shape[0])]
    for c in copies: c.start()
    for c in copies: c.wait()

def place(position,tiles,slots):
    return pl.pallas_call(place_kernel,
        out_shape=jax.ShapeDtypeStruct((slots,TILE,TILE),jnp.float32),
        in_specs=[pl.BlockSpec(memory_space=pltpu.SMEM),HBM],out_specs=HBM,
        scratch_shapes=[pltpu.SemaphoreType.DMA((tiles.shape[0],))],name="place")(position,tiles)

def subtract_kernel(per_step,labels,received,rows,out):
    t=pl.program_id(0)
    @pl.when(t==0)
    def _():
        for p in range(PB):
            out[p]=rows[p*TILE:(p+1)*TILE,:]
    def one(i,carry):
        label=labels[t*per_step+i]
        @pl.when(label>=0)
        def _():
            slot=label//2
            columns=pl.ds(pl.multiple_of((label-slot*2)*TILE,TILE),TILE)
            out[slot,:,columns]=out[slot,:,columns]-received[i]
        return carry
    lax.fori_loop(0,per_step,one,0)

def subtract(labels,received,rows,per_step=16):
    slots=received.shape[0]; width=rows.shape[1]
    return pl.pallas_call(functools.partial(subtract_kernel,per_step),
        out_shape=jax.ShapeDtypeStruct((PB,TILE,width),jnp.float32),
        grid_spec=pltpu.PrefetchScalarGridSpec(num_scalar_prefetch=1,grid=(slots//per_step,),
            in_specs=[pl.BlockSpec((per_step,TILE,TILE),lambda t,lab:(t,0,0)),
                      pl.BlockSpec((PB*TILE,width),lambda t,lab:(0,0))],
            out_specs=pl.BlockSpec((PB,TILE,width),lambda t,lab:(0,0,0))),
        name="subtract")(labels,received,rows)

def sum_parent(cross,row_pick,column_picks,parent_diag,fronts,blocks):
    height=parent_diag.shape[0]
    picked=lambda pick: jnp.stack([jnp.where(pick==0,1.0,0.0),jnp.where(pick==1,1.0,0.0)]).astype(jnp.float32)
    spread=cross.reshape(1,TILE,blocks,1,TILE)*picked(row_pick).reshape(2,1,1,1,1)*picked(column_picks).T.reshape(1,1,blocks,2,1)
    pieces=spread.reshape(fronts,height//fronts,W)
    mine=lax.all_to_all(pieces,"front",split_axis=0,concat_axis=0,tiled=True).sum(0)
    me=lax.axis_index("front")
    part=lax.dynamic_slice_in_dim(parent_diag,me*(height//fronts),height//fronts,0)-mine
    quarter=lax.all_to_all(jnp.broadcast_to(part[None],(fronts,)+part.shape),"front",split_axis=0,concat_axis=0,tiled=True)
    quarter=quarter.reshape(height,W)
    return lax.all_to_all(jnp.broadcast_to(quarter[None],(blocks,)+quarter.shape),"blk",split_axis=0,concat_axis=0,tiled=True).reshape(W,W)

def shards(child_diag,child_top,child_rows,row_owner,row_slot,col_block,parent_diag,parent_rows):
    blocks=lax.axis_size("blk"); fronts=lax.axis_size("front")
    my_block=lax.axis_index("blk")
    quarter=W//(TILE*blocks)
    capacity=2
    owners=row_owner[0,:,0]
    column_picks=col_block[0]
    block_ids=jnp.arange(blocks,dtype=jnp.int32)
    my_pick=jnp.sum(jnp.where(block_ids==my_block,column_picks,0))
    sequence=jnp.arange(owners.shape[0],dtype=jnp.int32)
    earlier=(owners[:,None]==owners[None,:])&(sequence[None,:]<sequence[:,None])
    position=owners*capacity+jnp.sum(earlier.astype(jnp.int32),axis=1)
    landing=row_slot[0]*quarter+my_pick
    hits=position[None,:]==jnp.arange(fronts*capacity,dtype=jnp.int32)[:,None]
    labels=jnp.max(jnp.where(hits,landing[None,:],-1),axis=1)
    labels=lax.all_to_all(labels.reshape(fronts,capacity),"front",split_axis=0,concat_axis=0,tiled=True).reshape(-1)
    diag_whole=lax.all_gather(child_diag,"blk",axis=0,tiled=True)
    top_whole=lax.all_gather(child_top,"blk",axis=0,tiled=True)
    schur,cross=child(diag_whole,top_whole,child_rows)
    arrived=lax.all_to_all(schur,"blk",split_axis=0,concat_axis=0,tiled=True).reshape(blocks*TA,TILE,TILE)
    outgoing=place(position,arrived,fronts*capacity)
    received=lax.all_to_all(outgoing.reshape(fronts,capacity,TILE,TILE),"front",split_axis=0,concat_axis=0,tiled=True)
    whole=sum_parent(cross,my_pick,column_picks,parent_diag,fronts,blocks)
    factor,inverse=parent(whole)
    updated=subtract(labels,received.reshape(-1,TILE,TILE),parent_rows)
    row_major=lax.all_to_all(updated,"blk",split_axis=0,concat_axis=2,tiled=True)
    row_major=row_major.reshape(TILE,W)
    height=parent_diag.shape[0]
    own=lax.dynamic_slice_in_dim(factor,my_block*height,height,0)
    panel=jnp.dot(row_major,inverse,precision=HIGHEST)
    return own,panel


def solution(mesh):
    return jax.shard_map(shards,mesh=mesh,
        in_specs=(P(("front","blk"),None),P(("front","blk"),None),P(("front","blk"),None),P("front",None,None),
                  P("front",None),P("front",None),P("blk",None),P("front","blk")),
        out_specs=(P("blk",None),P(("front","blk"),None)),check_vma=False)
```

```python
import functools
import jax
import jax.numpy as jnp
from jax import lax
from jax.experimental import pallas as pl
from jax.experimental.pallas import tpu as pltpu
from jax.sharding import PartitionSpec as P

W = 1024
TILE = 128
TA = 4
PB = 4
SUB = 8
HIGHEST=lax.Precision.HIGHEST
NT=(((1,),(1,)),((),()))

def dot_nt(a,b):
    return lax.dot_general(a,b,NT,precision=HIGHEST,preferred_element_type=jnp.float32)

def split(x):
    hi=x.astype(jnp.bfloat16)
    lo=(x-hi.astype(jnp.float32)).astype(jnp.bfloat16)
    return hi,lo

def dot3(ah,al,bh,bl):
    f=lambda p,q: lax.dot_general(p,q,NT,preferred_element_type=jnp.float32)
    return f(ah,bh)+(f(ah,bl)+f(al,bh))

def recip(x):
    r=pl.reciprocal(x,approx=True)
    r=r*(2.0-x*r)
    return r*(2.0-x*r)

def diag_steps(s):
    lane=lax.broadcasted_iota(jnp.int32,(SUB,TILE),1)
    sub=lax.broadcasted_iota(jnp.int32,(SUB,TILE),0)
    full=(SUB,TILE)
    for b in range(TILE//SUB):
        r0=b*SUB
        inside=(lane>=r0)&(lane<r0+SUB)
        v=[jnp.broadcast_to(s[r0+i:r0+i+1,:],full) for i in range(SUB)]
        a=[[jnp.broadcast_to(v[i][:,r0+j:r0+j+1],full) for j in range(i+1)] for i in range(SUB)]
        w=[jnp.where(inside,jnp.where(lane==r0+i,1.0,0.0),v[i]) for i in range(SUB)]
        r=[None]*SUB
        l=[[None]*SUB for _ in range(SUB)]
        for i in range(SUB):
            r[i]=recip(a[i][i])
            for k in range(i+1,SUB):
                l[k][i]=a[k][i]*r[i]
            for k in range(i+1,SUB):
                for m in range(i+1,k+1):
                    a[k][m]=a[k][m]-l[k][i]*a[m][i]
            for k in range(i+1,SUB):
                w[k]=w[k]-l[k][i]*w[i]
        z=[w[i]*r[i] for i in range(SUB)]
        for i in range(SUB-1,0,-1):
            for k in range(i):
                z[k]=z[k]-l[i][k]*z[i]
        for rb in range(b+1,TILE//SUB):
            x=s[rb*SUB:(rb+1)*SUB,:]
            c=[jnp.broadcast_to(x[:,r0+i:r0+i+1],full) for i in range(SUB)]
            p=c[0]*z[0]
            q=c[1]*z[1]
            for i in range(2,SUB,2):
                p=p+c[i]*z[i]
                q=q+c[i+1]*z[i+1]
            s[rb*SUB:(rb+1)*SUB,:]=jnp.where(inside,0.0,x)-(p+q)
        o=w[0]*lax.rsqrt(a[0][0])
        for i in range(1,SUB):
            o=jnp.where(sub==i,w[i]*lax.rsqrt(a[i][i]),o)
        s[r0:r0+SUB,:]=jnp.where(lane<r0+SUB,o,0.0)
        yield b

def diag(s):
    for _ in diag_steps(s): pass


def block(start,size=TILE):
    return pl.ds(pl.multiple_of(start,TILE),size)

def pieces(start,stop,size=256):
    return [slice(r,min(r+size,stop)) for r in range(start,stop,size)]

def chol_solve(m,x,n,e,s,inv_hi,inv_lo,p_hi,p_lo,low=None):
    s[...]=m[0:TILE,0:TILE]
    if low is not None:
        low[...]=jnp.zeros((W,W),jnp.float32)
        low[0:TILE,0:TILE]=m[0:TILE,0:TILE]
    e[...]=jnp.zeros((W,W),jnp.float32)
    diag(s)
    steps=TILE//SUB
    for c0 in range(0,W,TILE):
        c1=c0+TILE
        inv=s[...]
        ih,il=split(inv)
        inv_hi[...]=ih; inv_lo[...]=il
        if low is not None:
            low[c0:c1,c0:c1]=dot_nt(low[c0:c1,c0:c1],inv)
        e[c0:c1,c0:c1]=inv.T
        if c1<W:
            p=dot_nt(m[c1:c1+TILE,c0:c1],inv)
            new=m[c1:c1+TILE,c1:c1+TILE]-dot_nt(p,p)
            s[...]=new
            if low is not None:
                low[c1:c1+TILE,c1:c1+TILE]=new
        def solved(ref,r):
            a,b=split(ref[r,c0:c1])
            q=dot3(a,b,inv_hi[...],inv_lo[...])
            return q,split(q)
        def panel(r):
            q,(a,b)=solved(m,r)
            p_hi[r,:]=a; p_lo[r,:]=b
            if low is not None:
                low[r,c0:c1]=q
        def trail(r):
            end=r.stop
            m[r,c1:end]=m[r,c1:end]-dot3(p_hi[r,:],p_lo[r,:],p_hi[c1:end,:],p_lo[c1:end,:])
        def other(ref,r):
            q,(a,b)=solved(ref,r)
            if c1<W:
                ref[r,c1:]=ref[r,c1:]-dot3(a,b,p_hi[c1:,:],p_lo[c1:,:])
            ref[r,c0:c1]=q
        def start(r):
            e[r,c1:]=-dot3(*split(e[r,c0:c1]),p_hi[c1:,:],p_lo[c1:,:])
        work=[functools.partial(panel,r) for r in pieces(c1,W)]
        work+=[functools.partial(trail,r) for r in pieces(c1,W)]
        work+=[functools.partial(other,x,r) for r in pieces(0,n)]
        work+=[functools.partial(other,e,r) for r in pieces(0,c0)]
        if c1<W:
            work+=[functools.partial(start,slice(c0,c1))]
            done=0
            for b in diag_steps(s):
                upto=(b+1)*len(work)//steps
                for f in work[done:upto]: f()
                done=upto
        else:
            for f in work: f()

def scratch():
    b=jnp.bfloat16
    return [pltpu.VMEM((TILE,TILE),jnp.float32),pltpu.VMEM((TILE,TILE),b),pltpu.VMEM((TILE,TILE),b),
            pltpu.VMEM((W,TILE),b),pltpu.VMEM((W,TILE),b)]

HBM=pl.BlockSpec(memory_space=pl.ANY)
VM=pl.BlockSpec(memory_space=pltpu.VMEM)

def parent_kernel(a_ref,low_ref,inv_ref,m,sem,*rest):
    c=pltpu.make_async_copy(a_ref,m,sem); c.start(); c.wait()
    chol_solve(m,None,0,inv_ref,*rest,low=low_ref)

MESH = pl.DeviceIdType.MESH

def greet(partners):
    barrier=pltpu.get_barrier_semaphore()
    for p in partners:
        pl.semaphore_signal(barrier,inc=1,device_id=p,device_id_type=MESH)
    pl.semaphore_wait(barrier,len(partners))

def gather_kernel(blocks,mine,whole,send,recv,pass_sem):
    front=lax.axis_index("front"); me=lax.axis_index("blk")
    to=lambda d: (front,lax.rem(me+d,blocks))
    greet([to(d) for d in range(1,blocks)])
    h=mine.shape[0]; half=h//2
    def move(k,part,d,first):
        rows=slice(part*half,(part+1)*half); width=h*k+half*(part+1)
        there=whole.at[k*h+part*half:k*h+(part+1)*half,0:width]
        sem=send.at[part,d] if first else pass_sem.at[part]
        return pltpu.make_async_remote_copy(src_ref=mine.at[rows,0:width] if first else there,dst_ref=there,
            send_sem=sem,recv_sem=recv.at[k,part],device_id=to(d),device_id_type=MESH)
    for k in range(blocks):
        @pl.when(me==k)
        def _():
            for part,d in ((1,1),(0,blocks-1),(0,1),(1,blocks-1)): move(k,part,d,True).start()
    for k in range(blocks):
        @pl.when(me==(k+1)%blocks)
        def _():
            c=move(k,1,1,False); c.wait_recv(); c.start()
        @pl.when(me==(k-1)%blocks)
        def _():
            c=move(k,0,blocks-1,False); c.wait_recv(); c.start()
    for k in range(blocks):
        @pl.when(me==(k+1)%blocks)
        def _():
            move(k,0,1,False).wait_recv(); move(k,1,1,False).wait_send()
        @pl.when(me==(k-1)%blocks)
        def _():
            move(k,1,1,False).wait_recv(); move(k,0,1,False).wait_send()
        @pl.when(me==(k+2)%blocks)
        def _():
            move(k,0,1,False).wait_recv(); move(k,1,1,False).wait_recv()
        @pl.when(me==k)
        def _():
            for part,d in ((1,1),(0,blocks-1),(0,1),(1,blocks-1)): move(k,part,d,True).wait_send()

def gather(mine,blocks):
    h=mine.shape[0]
    return pl.pallas_call(functools.partial(gather_kernel,blocks),
        out_shape=jax.ShapeDtypeStruct((h*blocks,W),jnp.float32),in_specs=[HBM],out_specs=HBM,
        scratch_shapes=[pltpu.SemaphoreType.DMA((2,blocks)),pltpu.SemaphoreType.DMA((blocks,2)),pltpu.SemaphoreType.DMA((2,))],
        compiler_params=pltpu.CompilerParams(collective_id=0,has_side_effects=True),name="gather_diag",
        cost_estimate=pl.CostEstimate(flops=0,bytes_accessed=2**23,transcendentals=0))(mine)

SEEN = (0, 2, 4, 5, 6, 7)

def total_kernel(cross,flags,pd,meta,out,everyone,msg,ra,a1,rb,a2,rc,g,sa,qa,sb,qb,sc,qc,sd,qd,se,qe,sf,qf,sg,qg,sm,qm):
    front=lax.axis_index("front"); k=lax.axis_index("blk")
    x=front//16; y=(front//4)%4; zl=(front//2)%2; core=front%2
    l=zl*2+core; pos=k*2+zl
    at=lambda x,y,l: (x*16+y*4+l)
    def by_l(d): return (at(x,y,(l+d)%4),k)
    def by_x(d): return (at((x+d)%4,y,l),k)
    def by_y(d): return (at(x,(y+d)%4,l),k)
    def by_z(d):
        q=(pos+d)%8
        return (at(x,y,(q%2)*2+core),q//2)
    sibling=(at(x,y,zl*2+1-core),k)
    greet([by_l(d) for d in range(1,4)]+[by_x(d) for d in range(1,4)]+[by_y(d) for d in range(1,4)]+[by_z(d) for d in range(1,8)]+[sibling])
    def describe(src,dst,s,q,who):
        return pltpu.make_async_remote_copy(src_ref=src,dst_ref=dst,send_sem=s,recv_sem=q,device_id=who,device_id_type=MESH)
    def send(src,dst,s,q,i,who):
        c=describe(src,dst,s.at[i],q.at[i],who)
        c.start()
        return c
    for i in range(4):
        msg[i,0:TILE,:]=cross[:,i*TILE:(i+1)*TILE]
        msg[i,TILE:TILE+8,:]=flags[i]
    everyone[x,y,l]=meta[...]
    cs=[send(msg.at[(l+d)%4],ra.at[d],sa,qa,d,by_l(d)) for d in range(1,4)]
    cs+=[send(everyone.at[x,y,l],everyone.at[x,y,l],sm,qm,d,by_l(d)) for d in range(1,4)]
    ra[0]=msg[l]
    for c in cs: c.wait()
    for u in range(2):
        for v in range(2):
            t=None
            for i in range(4):
                p=ra[i,0:TILE,:]*ra[i,TILE+2*u+v:TILE+2*u+v+1,:]
                t=p if t is None else t+p
            a1[u,:,v*TILE:(v+1)*TILE]=t
    rows=lambda q,n: pl.ds(pl.multiple_of(q*n,n),n)
    cs=[send(a1.at[:,rows((x+d)%4,32),:],rb.at[d],sb,qb,d,by_x(d)) for d in range(1,4)]
    cs+=[send(everyone.at[x,y],everyone.at[x,y],sm,qm,d+4,by_x(d)) for d in range(1,4)]
    rb[0]=a1[:,rows(x,32),:]
    for c in cs: c.wait()
    a2[...]=(rb[0]+rb[1])+(rb[2]+rb[3])
    cs=[send(a2.at[:,rows((y+d)%4,8),:],rc.at[d],sc,qc,d,by_y(d)) for d in range(1,4)]
    ms=[send(everyone.at[:,y],everyone.at[:,y],sm,qm,d+8,by_y(d)) for d in range(1,4)]
    rc[0]=a2[:,rows(y,8),:]
    for c in cs: c.wait()
    t=(rc[0]+rc[1])+(rc[2]+rc[3])
    for i,q in enumerate(SEEN):
        @pl.when(pos==q)
        def _():
            for u in range(2):
                g[core,x,y,i,u]=pd[pl.ds(pl.multiple_of(u*TILE+(x*4+y)*8,8),8),pl.ds(pl.multiple_of(l*2*TILE,TILE),2*TILE)]-t[u]
            for d in range(1,8):
                describe(g.at[core,x,y,i],g.at[core,x,y,i],sd.at[d],qd.at[i],by_z(d)).start()
    for i,q in enumerate(SEEN):
        @pl.when(pos!=q)
        def _():
            describe(g.at[core,x,y,i],g.at[core,x,y,i],sd.at[0],qd.at[i],by_z(1)).wait_recv()
    for i,q in enumerate(SEEN):
        @pl.when(pos==q)
        def _():
            for d in range(1,8):
                describe(g.at[core,x,y,i],g.at[core,x,y,i],sd.at[d],qd.at[i],by_z(d)).wait_send()
    lo=pl.ds(0,3); hi=pl.ds(3,3)
    part=lambda a,b,h: g.at[core,a,b,h]
    es=[send(part(x,y,lo),part(x,y,lo),se,qe,d,by_x(d)) for d in range(1,4)]
    es+=[send(part(x,y,hi),part(x,y,hi),se,qe,d+4,by_y(d)) for d in range(1,4)]
    for c in es: c.wait()
    row=lambda b: g.at[core,:,b,lo]
    column=lambda a: g.at[core,a,:,hi]
    fs=[send(row(y),row(y),sf,qf,d,by_y(d)) for d in range(1,4)]
    fs+=[send(column(x),column(x),sf,qf,d+4,by_x(d)) for d in range(1,4)]
    gs=[send(row(y),row(y),sg,qg,0,sibling),send(column(x),column(x),sg,qg,4,sibling)]
    for d in range(1,4):
        fs[d-1].wait_recv()
        gs.append(send(row((y-d+4)%4),row((y-d+4)%4),sg,qg,d,sibling))
        fs[d+2].wait_recv()
        gs.append(send(column((x-d+4)%4),column((x-d+4)%4),sg,qg,d+4,sibling))
    for c in fs: c.wait_send()
    for c in ms: c.wait()
    for c in gs: c.wait()
    def assemble(i,carry):
        a=i//4; b=i%4
        for o in range(2):
            for n,q in enumerate(SEEN):
                for u in range(2):
                    c0=((q%2)*2+o)*2*TILE
                    out[pl.ds(pl.multiple_of((q//2*2+u)*TILE+i*8,8),8),c0:c0+2*TILE]=g[o,a,b,n,u]
        return carry
    lax.fori_loop(0,16,assemble,0)

def total(cross,flags,parent_diag,meta):
    f32=lambda *s: pltpu.VMEM(s,jnp.float32)
    sem=lambda n: pltpu.SemaphoreType.DMA((n,))
    return pl.pallas_call(total_kernel,
        out_shape=(jax.ShapeDtypeStruct((W,W),jnp.float32),jax.ShapeDtypeStruct((4,4,4,8,TILE),jnp.int32)),
        in_specs=[VM]*4,out_specs=(VM,VM),
        scratch_shapes=[f32(4,TILE+8,TILE),f32(4,TILE+8,TILE),f32(2,TILE,2*TILE),f32(4,2,32,2*TILE),f32(2,32,2*TILE),f32(4,2,8,2*TILE),
          f32(2,4,4,6,2,8,2*TILE)]+[sem(4)]*6+[sem(8)]*8+[sem(12)]*2,
        compiler_params=pltpu.CompilerParams(collective_id=1,has_side_effects=True,vmem_limit_bytes=32*2**20),name="total",
        cost_estimate=pl.CostEstimate(flops=0,bytes_accessed=2**26,transcendentals=0))(cross,flags,parent_diag,meta)

def factor_kernel(own_ref,whole_ref,rows_ref,xh_ref,xl_ref,ih_ref,il_ref,m,x,e,sems,*rest):
    n=rows_ref.shape[0]; h=own_ref.shape[0]; blocks=W//h
    me=lax.axis_index("blk")
    cp=[pltpu.make_async_copy(own_ref,m.at[pl.ds(pl.multiple_of(me*h,h),h),:],sems.at[0])]
    for d in range(1,blocks):
        r=pl.ds(pl.multiple_of(lax.rem(me+d,blocks)*h,h),h)
        cp.append(pltpu.make_async_copy(whole_ref.at[r,:],m.at[r,:],sems.at[d]))
    cp.append(pltpu.make_async_copy(rows_ref,x,sems.at[blocks]))
    for c in cp: c.start()
    for c in cp: c.wait()
    chol_solve(m,x,n,e,*rest)
    for i in range(n//TILE):
        r=slice(i*TILE,(i+1)*TILE)
        a,b=split(x[r,:]); xh_ref[r,:]=a; xl_ref[r,:]=b
    for i in range(W//TILE):
        r=slice(i*TILE,(i+1)*TILE)
        a,b=split(e[r,:]); ih_ref[r,:]=a; il_ref[r,:]=b

def factor_child(own,whole,rows):
    n=rows.shape[0]
    b=lambda r: jax.ShapeDtypeStruct((r,W),jnp.bfloat16)
    return pl.pallas_call(factor_kernel,out_shape=(b(n),b(n),b(W),b(W)),in_specs=[HBM]*3,out_specs=(VM,)*4,
        scratch_shapes=[pltpu.VMEM((W,W),jnp.float32),pltpu.VMEM((n,W),jnp.float32),pltpu.VMEM((W,W),jnp.float32),
          pltpu.SemaphoreType.DMA((8,))]+scratch(),
        compiler_params=pltpu.CompilerParams(vmem_limit_bytes=50*2**20),name="factor_child",
        cost_estimate=pl.CostEstimate(flops=2**36,bytes_accessed=2**24,transcendentals=0))(own,whole,rows)

def dot3n(ah,al,bh,bl):
    f=lambda p,q: jnp.dot(p,q,preferred_element_type=jnp.float32)
    return f(ah,bh)+(f(ah,bl)+f(al,bh))

def schur_kernel(top_ref,xh,xl,ih,il,schur_ref,cross_ref,t,th,tl):
    T=top_ref.shape[0]; n=xh.shape[0]
    for k in range(T//TILE):
        r=slice(k*TILE,(k+1)*TILE)
        a,b=split(top_ref[r,:])
        y=dot3n(a,b,ih[...],il[...])
        t[r,:]=y
        a,b=split(y); th[r,:]=a; tl[r,:]=b
    me=lax.axis_index("blk")
    cross_ref[...]=dot_nt(t[pl.ds(pl.multiple_of(me*TILE,TILE),TILE),:],t[...])
    for k in range(n//TILE):
        r=slice(k*TILE,(k+1)*TILE)
        y=dot3(xh[r,:],xl[r,:],th[...],tl[...])
        for q in range(T//TILE):
            schur_ref[q,r,:]=y[:,q*TILE:(q+1)*TILE]

def schur_tiles(top,xh,xl,ih,il):
    T=top.shape[0]; n=xh.shape[0]
    return pl.pallas_call(schur_kernel,
        out_shape=(jax.ShapeDtypeStruct((T//TILE,n,TILE),jnp.float32),jax.ShapeDtypeStruct((TILE,T),jnp.float32)),
        in_specs=[VM]*5,out_specs=(VM,VM),
        scratch_shapes=[pltpu.VMEM((T,W),jnp.float32),pltpu.VMEM((T,W),jnp.bfloat16),pltpu.VMEM((T,W),jnp.bfloat16)],
        compiler_params=pltpu.CompilerParams(vmem_limit_bytes=40*2**20),name="schur_tiles",
        cost_estimate=pl.CostEstimate(flops=2**33,bytes_accessed=2**24,transcendentals=0))(top,xh,xl,ih,il)

def parent(a):
    return pl.pallas_call(parent_kernel,
        out_shape=(jax.ShapeDtypeStruct((W,W),jnp.float32),)*2,
        in_specs=[HBM],out_specs=(VM,VM),
        scratch_shapes=[pltpu.VMEM((W,W),jnp.float32),pltpu.SemaphoreType.DMA]+scratch(),
        compiler_params=pltpu.CompilerParams(vmem_limit_bytes=56*2**20),name="parent",
        cost_estimate=pl.CostEstimate(flops=6*2**30,bytes_accessed=2**24,transcendentals=0))(a)

def place_kernel(position,tiles,out,sems):
    copies=[pltpu.make_async_copy(tiles.at[i],out.at[position[i]],sems.at[i]) for i in range(tiles.shape[0])]
    for c in copies: c.start()
    for c in copies: c.wait()

def place(position,tiles,slots):
    return pl.pallas_call(place_kernel,
        out_shape=jax.ShapeDtypeStruct((slots,TILE,TILE),jnp.float32),
        in_specs=[pl.BlockSpec(memory_space=pltpu.SMEM),VM],out_specs=HBM,
        scratch_shapes=[pltpu.SemaphoreType.DMA((tiles.shape[0],))],name="place")(position,tiles)

def subtract_kernel(per_step,labels,received,rows,out):
    t=pl.program_id(0)
    @pl.when(t==0)
    def _():
        for p in range(PB):
            out[p]=rows[p*TILE:(p+1)*TILE,:]
    def one(i,carry):
        label=labels[t*per_step+i]
        @pl.when(label>=0)
        def _():
            slot=label//2
            columns=pl.ds(pl.multiple_of((label-slot*2)*TILE,TILE),TILE)
            out[slot,:,columns]=out[slot,:,columns]-received[i]
        return carry
    lax.fori_loop(0,per_step,one,0)

def subtract(labels,received,rows,per_step=16):
    slots=received.shape[0]; width=rows.shape[1]
    return pl.pallas_call(functools.partial(subtract_kernel,per_step),
        out_shape=jax.ShapeDtypeStruct((PB,TILE,width),jnp.float32),
        grid_spec=pltpu.PrefetchScalarGridSpec(num_scalar_prefetch=1,grid=(slots//per_step,),
            in_specs=[pl.BlockSpec((per_step,TILE,TILE),lambda t,lab:(t,0,0)),
                      pl.BlockSpec((PB*TILE,width),lambda t,lab:(0,0))],
            out_specs=pl.BlockSpec((PB,TILE,width),lambda t,lab:(0,0,0))),
        name="subtract")(labels,received,rows)

def shards(child_diag,child_top,child_rows,row_owner,row_slot,col_block,parent_diag,parent_rows):
    blocks=lax.axis_size("blk"); fronts=lax.axis_size("front")
    my_block=lax.axis_index("blk")
    quarter=W//(TILE*blocks)
    capacity=2
    owners=row_owner[0,:,0]
    column_picks=col_block[0]
    block_ids=jnp.arange(blocks,dtype=jnp.int32)
    my_pick=jnp.sum(jnp.where(block_ids==my_block,column_picks,0))
    sequence=jnp.arange(owners.shape[0],dtype=jnp.int32)
    earlier=(owners[:,None]==owners[None,:])&(sequence[None,:]<sequence[:,None])
    position=owners*capacity+jnp.sum(earlier.astype(jnp.int32),axis=1)
    diag_whole=gather(child_diag,blocks)
    my_top,diag_whole=lax.optimization_barrier((child_top,diag_whole))
    top_whole=lax.all_gather(my_top,"blk",axis=0,tiled=True)
    schur,cross=schur_tiles(top_whole,*factor_child(child_diag,diag_whole,child_rows))
    arrived=lax.all_to_all(schur,"blk",split_axis=0,concat_axis=0,tiled=True).reshape(blocks*TA,TILE,TILE)
    outgoing=place(position,arrived,fronts*capacity)
    received=lax.all_to_all(outgoing.reshape(fronts,capacity,TILE,TILE),"front",split_axis=0,concat_axis=0,tiled=True)
    pairs=jnp.arange(8,dtype=jnp.int32)
    flags=(pairs[None,:]//2==my_pick)&(pairs[None,:]%2==column_picks[:,None])&(pairs[None,:]<4)
    flags=jnp.broadcast_to(flags.astype(jnp.float32)[:,:,None],(blocks,8,TILE))
    meta=jnp.zeros((8,TILE),jnp.int32).at[0,0:owners.shape[0]].set(owners).at[1,0:owners.shape[0]].set(row_slot[0])
    meta=meta.at[2,0:blocks].set(column_picks)
    whole,everyone=total(cross,flags,parent_diag,meta)
    everyone=everyone.reshape(fronts,8,TILE)
    all_owners=everyone[:,0,0:owners.shape[0]]
    ours=all_owners==lax.axis_index("front")
    nth=jnp.sum((ours[:,None,:]&(sequence[None,None,:]<sequence[None,:,None])).astype(jnp.int32),axis=2)
    their_pick=jnp.sum(jnp.where(block_ids==my_block,everyone[:,2,0:blocks],0),axis=1)
    landing=everyone[:,1,0:owners.shape[0]]*quarter+their_pick[:,None]
    turn=jnp.arange(capacity,dtype=jnp.int32)
    labels=jnp.max(jnp.where(ours[:,None,:]&(nth[:,None,:]==turn[None,:,None]),landing[:,None,:],-1),axis=2).reshape(-1)
    factor,inverse=parent(whole)
    received,inverse,factor=lax.optimization_barrier((received,inverse,factor))
    updated=subtract(labels,received.reshape(-1,TILE,TILE),parent_rows)
    row_major=lax.all_to_all(updated,"blk",split_axis=0,concat_axis=2,tiled=True)
    row_major=row_major.reshape(TILE,W)
    height=parent_diag.shape[0]
    own=lax.dynamic_slice_in_dim(factor,my_block*height,height,0)
    panel=jnp.dot(row_major,inverse,precision=HIGHEST)
    return own,panel


def solution(mesh):
    return jax.shard_map(shards,mesh=mesh,
        in_specs=(P(("front","blk"),None),P(("front","blk"),None),P(("front","blk"),None),P("front",None,None),
                  P("front",None),P("front",None),P("blk",None),P("front","blk")),
        out_specs=(P("blk",None),P(("front","blk"),None)),check_vma=False)
```

```python
import functools
import jax
import jax.numpy as jnp
from jax import lax
from jax.experimental import pallas as pl
from jax.experimental.pallas import tpu as pltpu
from jax.sharding import PartitionSpec as P

W = 1024
TILE = 128
TA = 4
PB = 4
SUB = 8
HIGHEST=lax.Precision.HIGHEST
NT=(((1,),(1,)),((),()))

def dot_nt(a,b):
    return lax.dot_general(a,b,NT,precision=HIGHEST,preferred_element_type=jnp.float32)

def split(x):
    hi=x.astype(jnp.bfloat16)
    lo=(x-hi.astype(jnp.float32)).astype(jnp.bfloat16)
    return hi,lo

def dot3(ah,al,bh,bl):
    f=lambda p,q: lax.dot_general(p,q,NT,preferred_element_type=jnp.float32)
    return f(ah,bh)+(f(ah,bl)+f(al,bh))

def recip(x):
    return pltpu.reciprocal(x,approx=True)

def diag_steps(s):
    lane=lax.broadcasted_iota(jnp.int32,(SUB,TILE),1)
    sub=lax.broadcasted_iota(jnp.int32,(SUB,TILE),0)
    full=(SUB,TILE)
    following=s[0:SUB,:]
    for b in range(TILE//SUB):
        r0=b*SUB
        inside=(lane>=r0)&(lane<r0+SUB)
        v=[jnp.broadcast_to(following[i:i+1,:],full) for i in range(SUB)]
        a=[[jnp.broadcast_to(v[i][:,r0+j:r0+j+1],full) for j in range(i+1)] for i in range(SUB)]
        w=[jnp.where(inside,jnp.where(lane==r0+i,1.0,0.0),v[i]) for i in range(SUB)]
        r=[None]*SUB
        l=[[None]*SUB for _ in range(SUB)]
        for i in range(SUB):
            r[i]=recip(a[i][i])
            for k in range(i+1,SUB):
                l[k][i]=a[k][i]*r[i]
            for k in range(i+1,SUB):
                for m in range(i+1,k+1):
                    a[k][m]=a[k][m]-l[k][i]*a[m][i]
            for k in range(i+1,SUB):
                w[k]=w[k]-l[k][i]*w[i]
        z=[w[i]*r[i] for i in range(SUB)]
        for i in range(SUB-1,0,-1):
            for k in range(i):
                z[k]=z[k]-l[i][k]*z[i]
        far=(b+2)*SUB
        if far<TILE:
            whole=z[0]
            for i in range(1,SUB): whole=jnp.where(sub==i,z[i],whole)
            x=s[far:,:]
            y=jnp.dot(x[:,r0:r0+SUB],whole,precision=HIGHEST,preferred_element_type=jnp.float32)
            rest=jnp.where(lax.broadcasted_iota(jnp.int32,x.shape,1)//SUB==b,0.0,x)-y
        if b+1<TILE//SUB:
            x=s[r0+SUB:far,:]
            c=[jnp.broadcast_to(x[:,r0+i:r0+i+1],full) for i in range(SUB)]
            p=c[0]*z[0]
            q=c[1]*z[1]
            for i in range(2,SUB,2):
                p=p+c[i]*z[i]
                q=q+c[i+1]*z[i+1]
            following=jnp.where(inside,0.0,x)-(p+q)
        if far<TILE:
            s[far:,:]=rest
        o=w[0]*lax.rsqrt(a[0][0])
        for i in range(1,SUB):
            o=jnp.where(sub==i,w[i]*lax.rsqrt(a[i][i]),o)
        s[r0:r0+SUB,:]=jnp.where(lane<r0+SUB,o,0.0)
        yield b

def diag(s):
    for _ in diag_steps(s): pass


def block(start,size=TILE):
    return pl.ds(pl.multiple_of(start,TILE),size)

def pieces(start,stop,size=256):
    return [slice(r,min(r+size,stop)) for r in range(start,stop,size)]

def chol_solve(m,x,n,e,s,inv_hi,inv_lo,p_hi,p_lo,low=None):
    s[...]=m[0:TILE,0:TILE]
    if low is not None:
        low[...]=jnp.zeros((W,W),jnp.float32)
        low[0:TILE,0:TILE]=m[0:TILE,0:TILE]
    e[...]=jnp.zeros((W,W),jnp.float32)
    diag(s)
    steps=TILE//SUB
    for c0 in range(0,W,TILE):
        c1=c0+TILE
        inv=s[...]
        ih,il=split(inv)
        inv_hi[...]=ih; inv_lo[...]=il
        if low is not None:
            low[c0:c1,c0:c1]=dot_nt(low[c0:c1,c0:c1],inv)
        e[c0:c1,c0:c1]=inv.T
        if c1<W:
            p=dot_nt(m[c1:c1+TILE,c0:c1],inv)
            new=m[c1:c1+TILE,c1:c1+TILE]-dot_nt(p,p)
            s[...]=new
            if low is not None:
                low[c1:c1+TILE,c1:c1+TILE]=new
        def solved(ref,r):
            a,b=split(ref[r,c0:c1])
            q=dot3(a,b,inv_hi[...],inv_lo[...])
            return q,split(q)
        def panel(r):
            q,(a,b)=solved(m,r)
            p_hi[r,:]=a; p_lo[r,:]=b
            if low is not None:
                low[r,c0:c1]=q
        def trail(r):
            end=r.stop
            m[r,c1:end]=m[r,c1:end]-dot3(p_hi[r,:],p_lo[r,:],p_hi[c1:end,:],p_lo[c1:end,:])
        def other(ref,r):
            q,(a,b)=solved(ref,r)
            if c1<W:
                ref[r,c1:]=ref[r,c1:]-dot3(a,b,p_hi[c1:,:],p_lo[c1:,:])
            ref[r,c0:c1]=q
        def start(r):
            e[r,c1:]=-dot3(*split(e[r,c0:c1]),p_hi[c1:,:],p_lo[c1:,:])
        work=[functools.partial(panel,r) for r in pieces(c1,W)]
        work+=[functools.partial(trail,r) for r in pieces(c1,W)]
        work+=[functools.partial(other,x,r) for r in pieces(0,n)]
        work+=[functools.partial(other,e,r) for r in pieces(0,c0)]
        if c1<W:
            work+=[functools.partial(start,slice(c0,c1))]
            done=0
            for b in diag_steps(s):
                upto=(b+1)*len(work)//steps
                for f in work[done:upto]: f()
                done=upto
        else:
            for f in work: f()

def scratch():
    b=jnp.bfloat16
    return [pltpu.VMEM((TILE,TILE),jnp.float32),pltpu.VMEM((TILE,TILE),b),pltpu.VMEM((TILE,TILE),b),
            pltpu.VMEM((W,TILE),b),pltpu.VMEM((W,TILE),b)]

HBM=pl.BlockSpec(memory_space=pl.ANY)
VM=pl.BlockSpec(memory_space=pltpu.VMEM)

def parent_kernel(a_ref,low_ref,inv_ref,m,sem,*rest):
    c=pltpu.make_async_copy(a_ref,m,sem); c.start(); c.wait()
    chol_solve(m,None,0,inv_ref,*rest,low=low_ref)

MESH = pl.DeviceIdType.MESH

def greet(partners):
    barrier=pltpu.get_barrier_semaphore()
    for p in partners:
        pl.semaphore_signal(barrier,inc=1,device_id=p,device_id_type=MESH)
    pl.semaphore_wait(barrier,len(partners))

def gather_kernel(blocks,mine,whole,send,recv,pass_sem):
    front=lax.axis_index("front"); me=lax.axis_index("blk")
    to=lambda d: (front,lax.rem(me+d,blocks))
    greet([to(d) for d in range(1,blocks)])
    h=mine.shape[0]; half=h//2
    def move(k,part,d,first):
        rows=slice(part*half,(part+1)*half); width=h*k+half*(part+1)
        there=whole.at[k*h+part*half:k*h+(part+1)*half,0:width]
        sem=send.at[part,d] if first else pass_sem.at[part]
        return pltpu.make_async_remote_copy(src_ref=mine.at[rows,0:width] if first else there,dst_ref=there,
            send_sem=sem,recv_sem=recv.at[k,part],device_id=to(d),device_id_type=MESH)
    for k in range(blocks):
        @pl.when(me==k)
        def _():
            for part,d in ((1,1),(0,blocks-1),(0,1),(1,blocks-1)): move(k,part,d,True).start()
    for k in range(blocks):
        @pl.when(me==(k+1)%blocks)
        def _():
            c=move(k,1,1,False); c.wait_recv(); c.start()
        @pl.when(me==(k-1)%blocks)
        def _():
            c=move(k,0,blocks-1,False); c.wait_recv(); c.start()
    for k in range(blocks):
        @pl.when(me==(k+1)%blocks)
        def _():
            move(k,0,1,False).wait_recv(); move(k,1,1,False).wait_send()
        @pl.when(me==(k-1)%blocks)
        def _():
            move(k,1,1,False).wait_recv(); move(k,0,1,False).wait_send()
        @pl.when(me==(k+2)%blocks)
        def _():
            move(k,0,1,False).wait_recv(); move(k,1,1,False).wait_recv()
        @pl.when(me==k)
        def _():
            for part,d in ((1,1),(0,blocks-1),(0,1),(1,blocks-1)): move(k,part,d,True).wait_send()

def gather(mine,blocks):
    h=mine.shape[0]
    return pl.pallas_call(functools.partial(gather_kernel,blocks),
        out_shape=jax.ShapeDtypeStruct((h*blocks,W),jnp.float32),in_specs=[HBM],out_specs=HBM,
        scratch_shapes=[pltpu.SemaphoreType.DMA((2,blocks)),pltpu.SemaphoreType.DMA((blocks,2)),pltpu.SemaphoreType.DMA((2,))],
        compiler_params=pltpu.CompilerParams(collective_id=0,has_side_effects=True),name="gather_diag",
        cost_estimate=pl.CostEstimate(flops=0,bytes_accessed=2**23,transcendentals=0))(mine)

SEEN = (0, 2, 4, 5, 6, 7)

def total_kernel(cross,flags,pd,meta,out,everyone,msg,ra,a1,rb,a2,rc,g,sa,qa,sb,qb,sc,qc,sd,qd,se,qe,sf,qf,sg,qg,sm,qm):
    front=lax.axis_index("front"); k=lax.axis_index("blk")
    x=front//16; y=(front//4)%4; zl=(front//2)%2; core=front%2
    l=zl*2+core; pos=k*2+zl
    at=lambda x,y,l: (x*16+y*4+l)
    def by_l(d): return (at(x,y,(l+d)%4),k)
    def by_x(d): return (at((x+d)%4,y,l),k)
    def by_y(d): return (at(x,(y+d)%4,l),k)
    def by_z(d):
        q=(pos+d)%8
        return (at(x,y,(q%2)*2+core),q//2)
    sibling=(at(x,y,zl*2+1-core),k)
    greet([by_l(d) for d in range(1,4)]+[by_x(d) for d in range(1,4)]+[by_y(d) for d in range(1,4)]+[by_z(d) for d in range(1,8)]+[sibling])
    def describe(src,dst,s,q,who):
        return pltpu.make_async_remote_copy(src_ref=src,dst_ref=dst,send_sem=s,recv_sem=q,device_id=who,device_id_type=MESH)
    def send(src,dst,s,q,i,who):
        c=describe(src,dst,s.at[i],q.at[i],who)
        c.start()
        return c
    for i in range(4):
        msg[i,0:TILE,:]=cross[:,i*TILE:(i+1)*TILE]
        msg[i,TILE:TILE+8,:]=flags[i]
    everyone[x,y,l]=meta[...]
    cs=[send(msg.at[(l+d)%4],ra.at[d],sa,qa,d,by_l(d)) for d in range(1,4)]
    cs+=[send(everyone.at[x,y,l],everyone.at[x,y,l],sm,qm,d,by_l(d)) for d in range(1,4)]
    ra[0]=msg[l]
    for c in cs: c.wait()
    for u in range(2):
        for v in range(2):
            t=None
            for i in range(4):
                p=ra[i,0:TILE,:]*ra[i,TILE+2*u+v:TILE+2*u+v+1,:]
                t=p if t is None else t+p
            a1[u,:,v*TILE:(v+1)*TILE]=t
    rows=lambda q,n: pl.ds(pl.multiple_of(q*n,n),n)
    cs=[send(a1.at[:,rows((x+d)%4,32),:],rb.at[d],sb,qb,d,by_x(d)) for d in range(1,4)]
    cs+=[send(everyone.at[x,y],everyone.at[x,y],sm,qm,d+4,by_x(d)) for d in range(1,4)]
    rb[0]=a1[:,rows(x,32),:]
    for c in cs: c.wait()
    a2[...]=(rb[0]+rb[1])+(rb[2]+rb[3])
    cs=[send(a2.at[:,rows((y+d)%4,8),:],rc.at[d],sc,qc,d,by_y(d)) for d in range(1,4)]
    ms=[send(everyone.at[:,y],everyone.at[:,y],sm,qm,d+8,by_y(d)) for d in range(1,4)]
    rc[0]=a2[:,rows(y,8),:]
    for c in cs: c.wait()
    t=(rc[0]+rc[1])+(rc[2]+rc[3])
    for i,q in enumerate(SEEN):
        @pl.when(pos==q)
        def _():
            for u in range(2):
                g[core,x,y,i,u]=pd[pl.ds(pl.multiple_of(u*TILE+(x*4+y)*8,8),8),pl.ds(pl.multiple_of(l*2*TILE,TILE),2*TILE)]-t[u]
            for d in range(1,8):
                describe(g.at[core,x,y,i],g.at[core,x,y,i],sd.at[d],qd.at[i],by_z(d)).start()
    for i,q in enumerate(SEEN):
        @pl.when(pos!=q)
        def _():
            describe(g.at[core,x,y,i],g.at[core,x,y,i],sd.at[0],qd.at[i],by_z(1)).wait_recv()
    for i,q in enumerate(SEEN):
        @pl.when(pos==q)
        def _():
            for d in range(1,8):
                describe(g.at[core,x,y,i],g.at[core,x,y,i],sd.at[d],qd.at[i],by_z(d)).wait_send()
    lo=pl.ds(0,3); hi=pl.ds(3,3)
    part=lambda a,b,h: g.at[core,a,b,h]
    es=[send(part(x,y,lo),part(x,y,lo),se,qe,d,by_x(d)) for d in range(1,4)]
    es+=[send(part(x,y,hi),part(x,y,hi),se,qe,d+4,by_y(d)) for d in range(1,4)]
    for c in es: c.wait()
    row=lambda b: g.at[core,:,b,lo]
    column=lambda a: g.at[core,a,:,hi]
    fs=[send(row(y),row(y),sf,qf,d,by_y(d)) for d in range(1,4)]
    fs+=[send(column(x),column(x),sf,qf,d+4,by_x(d)) for d in range(1,4)]
    gs=[send(row(y),row(y),sg,qg,0,sibling),send(column(x),column(x),sg,qg,4,sibling)]
    for d in range(1,4):
        fs[d-1].wait_recv()
        gs.append(send(row((y-d+4)%4),row((y-d+4)%4),sg,qg,d,sibling))
        fs[d+2].wait_recv()
        gs.append(send(column((x-d+4)%4),column((x-d+4)%4),sg,qg,d+4,sibling))
    for c in fs: c.wait_send()
    for c in ms: c.wait()
    for c in gs: c.wait()
    def assemble(i,carry):
        a=i//4; b=i%4
        for o in range(2):
            for n,q in enumerate(SEEN):
                for u in range(2):
                    c0=((q%2)*2+o)*2*TILE
                    out[pl.ds(pl.multiple_of((q//2*2+u)*TILE+i*8,8),8),c0:c0+2*TILE]=g[o,a,b,n,u]
        return carry
    lax.fori_loop(0,16,assemble,0)

def total(cross,flags,parent_diag,meta):
    f32=lambda *s: pltpu.VMEM(s,jnp.float32)
    sem=lambda n: pltpu.SemaphoreType.DMA((n,))
    return pl.pallas_call(total_kernel,
        out_shape=(jax.ShapeDtypeStruct((W,W),jnp.float32),jax.ShapeDtypeStruct((4,4,4,8,TILE),jnp.int32)),
        in_specs=[VM]*4,out_specs=(VM,VM),
        scratch_shapes=[f32(4,TILE+8,TILE),f32(4,TILE+8,TILE),f32(2,TILE,2*TILE),f32(4,2,32,2*TILE),f32(2,32,2*TILE),f32(4,2,8,2*TILE),
          f32(2,4,4,6,2,8,2*TILE)]+[sem(4)]*6+[sem(8)]*8+[sem(12)]*2,
        compiler_params=pltpu.CompilerParams(collective_id=1,has_side_effects=True,vmem_limit_bytes=32*2**20),name="total",
        cost_estimate=pl.CostEstimate(flops=0,bytes_accessed=2**26,transcendentals=0))(cross,flags,parent_diag,meta)

def factor_kernel(own_ref,whole_ref,rows_ref,xh_ref,xl_ref,ih_ref,il_ref,m,x,e,sems,*rest):
    n=rows_ref.shape[0]; h=own_ref.shape[0]; blocks=W//h
    me=lax.axis_index("blk")
    cp=[pltpu.make_async_copy(own_ref,m.at[pl.ds(pl.multiple_of(me*h,h),h),:],sems.at[0])]
    for d in range(1,blocks):
        r=pl.ds(pl.multiple_of(lax.rem(me+d,blocks)*h,h),h)
        cp.append(pltpu.make_async_copy(whole_ref.at[r,:],m.at[r,:],sems.at[d]))
    cp.append(pltpu.make_async_copy(rows_ref,x,sems.at[blocks]))
    for c in cp: c.start()
    for c in cp: c.wait()
    chol_solve(m,x,n,e,*rest)
    for i in range(n//TILE):
        r=slice(i*TILE,(i+1)*TILE)
        a,b=split(x[r,:]); xh_ref[r,:]=a; xl_ref[r,:]=b
    for i in range(W//TILE):
        r=slice(i*TILE,(i+1)*TILE)
        a,b=split(e[r,:]); ih_ref[r,:]=a; il_ref[r,:]=b

def factor_child(own,whole,rows):
    n=rows.shape[0]
    b=lambda r: jax.ShapeDtypeStruct((r,W),jnp.bfloat16)
    return pl.pallas_call(factor_kernel,out_shape=(b(n),b(n),b(W),b(W)),in_specs=[HBM]*3,out_specs=(VM,)*4,
        scratch_shapes=[pltpu.VMEM((W,W),jnp.float32),pltpu.VMEM((n,W),jnp.float32),pltpu.VMEM((W,W),jnp.float32),
          pltpu.SemaphoreType.DMA((8,))]+scratch(),
        compiler_params=pltpu.CompilerParams(vmem_limit_bytes=56*2**20),name="factor_child",
        cost_estimate=pl.CostEstimate(flops=2**36,bytes_accessed=2**24,transcendentals=0))(own,whole,rows)

def dot3n(ah,al,bh,bl):
    f=lambda p,q: jnp.dot(p,q,preferred_element_type=jnp.float32)
    return f(ah,bh)+(f(ah,bl)+f(al,bh))

def schur_kernel(*refs):
    operands,(schur_ref,cross_ref,t,th,tl),loaded,sems=refs[:5],refs[5:10],refs[10:15],refs[15]
    copies=[pltpu.make_async_copy(a,b,sems.at[i]) for i,(a,b) in enumerate(zip(operands,loaded))]
    for c in copies: c.start()
    top_ref,xh,xl,ih,il=loaded
    T=top_ref.shape[0]; n=xh.shape[0]
    for i in (0,3,4): copies[i].wait()
    for k in range(T//TILE):
        r=slice(k*TILE,(k+1)*TILE)
        a,b=split(top_ref[r,:])
        y=dot3n(a,b,ih[...],il[...])
        t[r,:]=y
        a,b=split(y); th[r,:]=a; tl[r,:]=b
    me=lax.axis_index("blk")
    cross_ref[...]=dot_nt(t[pl.ds(pl.multiple_of(me*TILE,TILE),TILE),:],t[...])
    for i in (1,2): copies[i].wait()
    for k in range(n//TILE):
        r=slice(k*TILE,(k+1)*TILE)
        y=dot3(xh[r,:],xl[r,:],th[...],tl[...])
        for q in range(T//TILE):
            schur_ref[q,r,:]=y[:,q*TILE:(q+1)*TILE]

def schur_tiles(top,xh,xl,ih,il):
    T=top.shape[0]; n=xh.shape[0]
    return pl.pallas_call(schur_kernel,
        out_shape=(jax.ShapeDtypeStruct((T//TILE,n,TILE),jnp.float32),jax.ShapeDtypeStruct((TILE,T),jnp.float32)),
        in_specs=[HBM]*5,out_specs=(VM,VM),
        scratch_shapes=[pltpu.VMEM((T,W),jnp.float32),pltpu.VMEM((T,W),jnp.bfloat16),pltpu.VMEM((T,W),jnp.bfloat16)]
          +[pltpu.VMEM(v.shape,v.dtype) for v in (top,xh,xl,ih,il)]+[pltpu.SemaphoreType.DMA((5,))],
        compiler_params=pltpu.CompilerParams(vmem_limit_bytes=56*2**20),name="schur_tiles",
        cost_estimate=pl.CostEstimate(flops=2**33,bytes_accessed=2**24,transcendentals=0))(top,xh,xl,ih,il)

def parent(a):
    return pl.pallas_call(parent_kernel,
        out_shape=(jax.ShapeDtypeStruct((W,W),jnp.float32),)*2,
        in_specs=[HBM],out_specs=(VM,VM),
        scratch_shapes=[pltpu.VMEM((W,W),jnp.float32),pltpu.SemaphoreType.DMA]+scratch(),
        compiler_params=pltpu.CompilerParams(vmem_limit_bytes=56*2**20),name="parent",
        cost_estimate=pl.CostEstimate(flops=6*2**30,bytes_accessed=2**24,transcendentals=0))(a)

def place_kernel(position,tiles,out,sems):
    copies=[pltpu.make_async_copy(tiles.at[i],out.at[position[i]],sems.at[i]) for i in range(tiles.shape[0])]
    for c in copies: c.start()
    for c in copies: c.wait()

def place(position,tiles,slots):
    return pl.pallas_call(place_kernel,
        out_shape=jax.ShapeDtypeStruct((slots,TILE,TILE),jnp.float32),
        in_specs=[pl.BlockSpec(memory_space=pltpu.SMEM),VM],out_specs=HBM,
        scratch_shapes=[pltpu.SemaphoreType.DMA((tiles.shape[0],))],name="place")(position,tiles)

def subtract_kernel(per_step,labels,received,rows,out):
    t=pl.program_id(0)
    @pl.when(t==0)
    def _():
        for p in range(PB):
            out[p]=rows[p*TILE:(p+1)*TILE,:]
    def one(i,carry):
        label=labels[t*per_step+i]
        @pl.when(label>=0)
        def _():
            slot=label//2
            columns=pl.ds(pl.multiple_of((label-slot*2)*TILE,TILE),TILE)
            out[slot,:,columns]=out[slot,:,columns]-received[i]
        return carry
    lax.fori_loop(0,per_step,one,0)

def subtract(labels,received,rows,per_step=16):
    slots=received.shape[0]; width=rows.shape[1]
    return pl.pallas_call(functools.partial(subtract_kernel,per_step),
        out_shape=jax.ShapeDtypeStruct((PB,TILE,width),jnp.float32),
        grid_spec=pltpu.PrefetchScalarGridSpec(num_scalar_prefetch=1,grid=(slots//per_step,),
            in_specs=[pl.BlockSpec((per_step,TILE,TILE),lambda t,lab:(t,0,0)),
                      pl.BlockSpec((PB*TILE,width),lambda t,lab:(0,0))],
            out_specs=pl.BlockSpec((PB,TILE,width),lambda t,lab:(0,0,0))),
        name="subtract")(labels,received,rows)

def shards(child_diag,child_top,child_rows,row_owner,row_slot,col_block,parent_diag,parent_rows):
    blocks=lax.axis_size("blk"); fronts=lax.axis_size("front")
    my_block=lax.axis_index("blk")
    quarter=W//(TILE*blocks)
    capacity=2
    owners=row_owner[0,:,0]
    column_picks=col_block[0]
    block_ids=jnp.arange(blocks,dtype=jnp.int32)
    my_pick=jnp.sum(jnp.where(block_ids==my_block,column_picks,0))
    sequence=jnp.arange(owners.shape[0],dtype=jnp.int32)
    earlier=(owners[:,None]==owners[None,:])&(sequence[None,:]<sequence[:,None])
    position=owners*capacity+jnp.sum(earlier.astype(jnp.int32),axis=1)
    diag_whole=gather(child_diag,blocks)
    my_top,diag_whole=lax.optimization_barrier((child_top,diag_whole))
    top_whole=lax.all_gather(my_top,"blk",axis=0,tiled=True)
    schur,cross=schur_tiles(top_whole,*factor_child(child_diag,diag_whole,child_rows))
    pairs=jnp.arange(8,dtype=jnp.int32)
    flags=(pairs[None,:]//2==my_pick)&(pairs[None,:]%2==column_picks[:,None])&(pairs[None,:]<4)
    flags=jnp.broadcast_to(flags.astype(jnp.float32)[:,:,None],(blocks,8,TILE))
    meta=jnp.zeros((8,TILE),jnp.int32).at[0,0:owners.shape[0]].set(owners).at[1,0:owners.shape[0]].set(row_slot[0])
    meta=meta.at[2,0:blocks].set(column_picks)
    whole,everyone=total(cross,flags,parent_diag,meta)
    arrived=lax.all_to_all(schur,"blk",split_axis=0,concat_axis=0,tiled=True).reshape(blocks*TA,TILE,TILE)
    arrived,whole,everyone=lax.optimization_barrier((arrived,whole,everyone))
    outgoing=place(position,arrived,fronts*capacity)
    received=lax.all_to_all(outgoing.reshape(fronts,capacity,TILE,TILE),"front",split_axis=0,concat_axis=0,tiled=True)
    everyone=everyone.reshape(fronts,8,TILE)
    all_owners=everyone[:,0,0:owners.shape[0]]
    ours=all_owners==lax.axis_index("front")
    nth=jnp.sum((ours[:,None,:]&(sequence[None,None,:]<sequence[None,:,None])).astype(jnp.int32),axis=2)
    their_pick=jnp.sum(jnp.where(block_ids==my_block,everyone[:,2,0:blocks],0),axis=1)
    landing=everyone[:,1,0:owners.shape[0]]*quarter+their_pick[:,None]
    turn=jnp.arange(capacity,dtype=jnp.int32)
    labels=jnp.max(jnp.where(ours[:,None,:]&(nth[:,None,:]==turn[None,:,None]),landing[:,None,:],-1),axis=2).reshape(-1)
    factor,inverse=parent(whole)
    received,inverse,factor=lax.optimization_barrier((received,inverse,factor))
    updated=subtract(labels,received.reshape(-1,TILE,TILE),parent_rows)
    row_major=lax.all_to_all(updated,"blk",split_axis=0,concat_axis=2,tiled=True)
    row_major=row_major.reshape(TILE,W)
    height=parent_diag.shape[0]
    own=lax.dynamic_slice_in_dim(factor,my_block*height,height,0)
    panel=jnp.dot(row_major,inverse,precision=HIGHEST)
    return own,panel


def solution(mesh):
    return jax.shard_map(shards,mesh=mesh,
        in_specs=(P(("front","blk"),None),P(("front","blk"),None),P(("front","blk"),None),P("front",None,None),
                  P("front",None),P("front",None),P("blk",None),P("front","blk")),
        out_specs=(P("blk",None),P(("front","blk"),None)),check_vma=False)
```

```python
import functools
import jax
import jax.numpy as jnp
from jax import lax
from jax.experimental import pallas as pl
from jax.experimental.pallas import tpu as pltpu
from jax.sharding import PartitionSpec as P

W = 1024
TILE = 128
TA = 4
PB = 4
SUB = 8
HIGHEST=lax.Precision.HIGHEST
NT=(((1,),(1,)),((),()))

def dot_nt(a,b):
    return lax.dot_general(a,b,NT,precision=HIGHEST,preferred_element_type=jnp.float32)

def split(x):
    hi=x.astype(jnp.bfloat16)
    lo=(x-hi.astype(jnp.float32)).astype(jnp.bfloat16)
    return hi,lo

def dot3(ah,al,bh,bl):
    f=lambda p,q: lax.dot_general(p,q,NT,preferred_element_type=jnp.float32)
    return f(ah,bh)+(f(ah,bl)+f(al,bh))

def recip(x):
    return pltpu.reciprocal(x,approx=True)

def diag_steps(s):
    lane=lax.broadcasted_iota(jnp.int32,(SUB,TILE),1)
    sub=lax.broadcasted_iota(jnp.int32,(SUB,TILE),0)
    full=(SUB,TILE)
    following=s[0:SUB,:]
    for b in range(TILE//SUB):
        r0=b*SUB
        inside=(lane>=r0)&(lane<r0+SUB)
        v=[jnp.broadcast_to(following[i:i+1,:],full) for i in range(SUB)]
        a=[[jnp.broadcast_to(v[i][:,r0+j:r0+j+1],full) for j in range(i+1)] for i in range(SUB)]
        w=[jnp.where(inside,jnp.where(lane==r0+i,1.0,0.0),v[i]) for i in range(SUB)]
        r=[None]*SUB
        l=[[None]*SUB for _ in range(SUB)]
        for i in range(SUB):
            r[i]=recip(a[i][i])
            for k in range(i+1,SUB):
                l[k][i]=a[k][i]*r[i]
            for k in range(i+1,SUB):
                for m in range(i+1,k+1):
                    a[k][m]=a[k][m]-l[k][i]*a[m][i]
            for k in range(i+1,SUB):
                w[k]=w[k]-l[k][i]*w[i]
        z=[w[i]*r[i] for i in range(SUB)]
        for i in range(SUB-1,0,-1):
            for k in range(i):
                z[k]=z[k]-l[i][k]*z[i]
        far=(b+2)*SUB
        if far<TILE:
            whole=z[0]
            for i in range(1,SUB): whole=jnp.where(sub==i,z[i],whole)
            x=s[far:,:]
            y=jnp.dot(x[:,r0:r0+SUB],whole,precision=HIGHEST,preferred_element_type=jnp.float32)
            rest=jnp.where(lax.broadcasted_iota(jnp.int32,x.shape,1)//SUB==b,0.0,x)-y
        if b+1<TILE//SUB:
            x=s[r0+SUB:far,:]
            c=[jnp.broadcast_to(x[:,r0+i:r0+i+1],full) for i in range(SUB)]
            p=c[0]*z[0]
            q=c[1]*z[1]
            for i in range(2,SUB,2):
                p=p+c[i]*z[i]
                q=q+c[i+1]*z[i+1]
            following=jnp.where(inside,0.0,x)-(p+q)
        if far<TILE:
            s[far:,:]=rest
        o=w[0]*lax.rsqrt(a[0][0])
        for i in range(1,SUB):
            o=jnp.where(sub==i,w[i]*lax.rsqrt(a[i][i]),o)
        s[r0:r0+SUB,:]=jnp.where(lane<r0+SUB,o,0.0)
        yield b

def diag(s):
    for _ in diag_steps(s): pass


def block(start,size=TILE):
    return pl.ds(pl.multiple_of(start,TILE),size)

def pieces(start,stop,size=256):
    return [slice(r,min(r+size,stop)) for r in range(start,stop,size)]

def chol_solve(m,x,n,e,s,inv_hi,inv_lo,p_hi,p_lo,low=None):
    s[...]=m[0:TILE,0:TILE]
    if low is not None:
        low[...]=jnp.zeros((W,W),jnp.float32)
        low[0:TILE,0:TILE]=m[0:TILE,0:TILE]
    e[...]=jnp.zeros((W,W),jnp.float32)
    diag(s)
    steps=TILE//SUB
    for c0 in range(0,W,TILE):
        c1=c0+TILE
        inv=s[...]
        ih,il=split(inv)
        inv_hi[...]=ih; inv_lo[...]=il
        if low is not None:
            low[c0:c1,c0:c1]=dot_nt(low[c0:c1,c0:c1],inv)
        e[c0:c1,c0:c1]=inv.T
        if c1<W:
            p=dot_nt(m[c1:c1+TILE,c0:c1],inv)
            new=m[c1:c1+TILE,c1:c1+TILE]-dot_nt(p,p)
            s[...]=new
            if low is not None:
                low[c1:c1+TILE,c1:c1+TILE]=new
        def solved(ref,r):
            a,b=split(ref[r,c0:c1])
            q=dot3(a,b,inv_hi[...],inv_lo[...])
            return q,split(q)
        def panel(r):
            q,(a,b)=solved(m,r)
            p_hi[r,:]=a; p_lo[r,:]=b
            if low is not None:
                low[r,c0:c1]=q
        def trail(r):
            end=r.stop
            m[r,c1:end]=m[r,c1:end]-dot3(p_hi[r,:],p_lo[r,:],p_hi[c1:end,:],p_lo[c1:end,:])
        def other(ref,r):
            q,(a,b)=solved(ref,r)
            if c1<W:
                ref[r,c1:]=ref[r,c1:]-dot3(a,b,p_hi[c1:,:],p_lo[c1:,:])
            ref[r,c0:c1]=q
        def start(r):
            e[r,c1:]=-dot3(*split(e[r,c0:c1]),p_hi[c1:,:],p_lo[c1:,:])
        work=[functools.partial(panel,r) for r in pieces(c1,W)]
        work+=[functools.partial(trail,r) for r in pieces(c1,W)]
        work+=[functools.partial(other,x,r) for r in pieces(0,n)]
        work+=[functools.partial(other,e,r) for r in pieces(0,c0)]
        if c1<W:
            work+=[functools.partial(start,slice(c0,c1))]
            done=0
            for b in diag_steps(s):
                upto=(b+1)*len(work)//steps
                for f in work[done:upto]: f()
                done=upto
        else:
            for f in work: f()

def scratch():
    b=jnp.bfloat16
    return [pltpu.VMEM((TILE,TILE),jnp.float32),pltpu.VMEM((TILE,TILE),b),pltpu.VMEM((TILE,TILE),b),
            pltpu.VMEM((W,TILE),b),pltpu.VMEM((W,TILE),b)]

HBM=pl.BlockSpec(memory_space=pl.ANY)
VM=pl.BlockSpec(memory_space=pltpu.VMEM)

def parent_kernel(a_ref,low_ref,inv_ref,m,sem,*rest):
    c=pltpu.make_async_copy(a_ref,m,sem); c.start(); c.wait()
    chol_solve(m,None,0,inv_ref,*rest,low=low_ref)

MESH = pl.DeviceIdType.MESH

def greet(partners):
    barrier=pltpu.get_barrier_semaphore()
    for p in partners:
        pl.semaphore_signal(barrier,inc=1,device_id=p,device_id_type=MESH)
    pl.semaphore_wait(barrier,len(partners))

PIECES = (
    ((0,0,1,1),(1,0,2,1)),
    ((0,0,3,-1),(1,0,4,-1)),
    ((0,2,5,-1),(1,0,3,-1),(1,3,6,-1),(0,0,2,1)),
    ((0,4,7,1),(1,0,4,1),(1,4,8,1),(0,0,4,-1)),
)

def gather_kernel(blocks,mine,whole,send,recv,pass_sem):
    front=lax.axis_index("front"); me=lax.axis_index("blk")
    to=lambda d: (front,lax.rem(me+d+blocks,blocks))
    greet([to(d) for d in range(1,blocks)])
    h=mine.shape[0]; half=h//2
    def move(k,i,d,first):
        part,a,b,_=PIECES[k][i]
        rows=slice(part*half,(part+1)*half); columns=slice(a*TILE,b*TILE)
        there=whole.at[k*h+part*half:k*h+(part+1)*half,columns]
        sem=send.at[i,(d+1)//2] if first else pass_sem.at[k,i]
        return pltpu.make_async_remote_copy(src_ref=mine.at[rows,columns] if first else there,dst_ref=there,
            send_sem=sem,recv_sem=recv.at[k,i],device_id=to(d),device_id_type=MESH)
    def order(k,d):
        count=range(len(PIECES[k]))
        return [i for i in count if PIECES[k][i][3]==d]+[i for i in count if PIECES[k][i][3]!=d]
    for k in range(blocks):
        @pl.when(me==k)
        def _():
            for a,b in zip(order(k,1),order(k,-1)):
                move(k,a,1,True).start(); move(k,b,-1,True).start()
    for i in range(4):
        for k in range(blocks):
            for d in (1,-1):
                if i<len(PIECES[k]) and PIECES[k][i][3]==d:
                    @pl.when(me==(k+d)%blocks)
                    def _():
                        c=move(k,i,d,False); c.wait_recv(); c.start()
    for k in range(blocks):
        for d in (1,-1):
            @pl.when(me==(k+d)%blocks)
            def _():
                for i in range(len(PIECES[k])):
                    if PIECES[k][i][3]==d: move(k,i,d,False).wait_send()
                    else: move(k,i,d,False).wait_recv()
        @pl.when(me==(k+2)%blocks)
        def _():
            for i in range(len(PIECES[k])): move(k,i,1,False).wait_recv()
        @pl.when(me==k)
        def _():
            for i in range(len(PIECES[k])):
                for d in (1,-1): move(k,i,d,True).wait_send()

def gather(mine,blocks):
    h=mine.shape[0]
    return pl.pallas_call(functools.partial(gather_kernel,blocks),
        out_shape=jax.ShapeDtypeStruct((h*blocks,W),jnp.float32),in_specs=[HBM],out_specs=HBM,
        scratch_shapes=[pltpu.SemaphoreType.DMA((4,2)),pltpu.SemaphoreType.DMA((blocks,4)),pltpu.SemaphoreType.DMA((blocks,4))],
        compiler_params=pltpu.CompilerParams(collective_id=0,has_side_effects=True),name="gather_diag",
        cost_estimate=pl.CostEstimate(flops=0,bytes_accessed=2**23,transcendentals=0))(mine)

SEEN = (0, 2, 4, 5, 6, 7)

def total_kernel(cross,flags,pd,meta,out,everyone,msg,ra,a1,rb,a2,rc,g,sa,qa,sb,qb,sc,qc,sd,qd,se,qe,sf,qf,sg,qg,sm,qm):
    front=lax.axis_index("front"); k=lax.axis_index("blk")
    x=front//16; y=(front//4)%4; zl=(front//2)%2; core=front%2
    l=zl*2+core; pos=k*2+zl
    at=lambda x,y,l: (x*16+y*4+l)
    def by_l(d): return (at(x,y,(l+d)%4),k)
    def by_x(d): return (at((x+d)%4,y,l),k)
    def by_y(d): return (at(x,(y+d)%4,l),k)
    def by_z(d):
        q=(pos+d)%8
        return (at(x,y,(q%2)*2+core),q//2)
    sibling=(at(x,y,zl*2+1-core),k)
    greet([by_l(d) for d in range(1,4)]+[by_x(d) for d in range(1,4)]+[by_y(d) for d in range(1,4)]+[by_z(d) for d in range(1,8)]+[sibling])
    def describe(src,dst,s,q,who):
        return pltpu.make_async_remote_copy(src_ref=src,dst_ref=dst,send_sem=s,recv_sem=q,device_id=who,device_id_type=MESH)
    def send(src,dst,s,q,i,who):
        c=describe(src,dst,s.at[i],q.at[i],who)
        c.start()
        return c
    for i in range(4):
        msg[i,0:TILE,:]=cross[:,i*TILE:(i+1)*TILE]
        msg[i,TILE:TILE+8,:]=flags[i]
    everyone[x,y,l]=meta[...]
    cs=[send(msg.at[(l+d)%4],ra.at[d],sa,qa,d,by_l(d)) for d in range(1,4)]
    cs+=[send(everyone.at[x,y,l],everyone.at[x,y,l],sm,qm,d,by_l(d)) for d in range(1,4)]
    ra[0]=msg[l]
    for c in cs: c.wait()
    for u in range(2):
        for v in range(2):
            t=None
            for i in range(4):
                p=ra[i,0:TILE,:]*ra[i,TILE+2*u+v:TILE+2*u+v+1,:]
                t=p if t is None else t+p
            a1[u,:,v*TILE:(v+1)*TILE]=t
    rows=lambda q,n: pl.ds(pl.multiple_of(q*n,n),n)
    cs=[send(a1.at[:,rows((x+d)%4,32),:],rb.at[d],sb,qb,d,by_x(d)) for d in range(1,4)]
    cs+=[send(everyone.at[x,y],everyone.at[x,y],sm,qm,d+4,by_x(d)) for d in range(1,4)]
    rb[0]=a1[:,rows(x,32),:]
    for c in cs: c.wait()
    a2[...]=(rb[0]+rb[1])+(rb[2]+rb[3])
    cs=[send(a2.at[:,rows((y+d)%4,8),:],rc.at[d],sc,qc,d,by_y(d)) for d in range(1,4)]
    ms=[send(everyone.at[:,y],everyone.at[:,y],sm,qm,d+8,by_y(d)) for d in range(1,4)]
    rc[0]=a2[:,rows(y,8),:]
    for c in cs: c.wait()
    t=(rc[0]+rc[1])+(rc[2]+rc[3])
    for i,q in enumerate(SEEN):
        @pl.when(pos==q)
        def _():
            for u in range(2):
                g[core,x,y,i,u]=pd[pl.ds(pl.multiple_of(u*TILE+(x*4+y)*8,8),8),pl.ds(pl.multiple_of(l*2*TILE,TILE),2*TILE)]-t[u]
            for d in range(1,8):
                describe(g.at[core,x,y,i],g.at[core,x,y,i],sd.at[d],qd.at[i],by_z(d)).start()
    for i,q in enumerate(SEEN):
        @pl.when(pos!=q)
        def _():
            describe(g.at[core,x,y,i],g.at[core,x,y,i],sd.at[0],qd.at[i],by_z(1)).wait_recv()
    for i,q in enumerate(SEEN):
        @pl.when(pos==q)
        def _():
            for d in range(1,8):
                describe(g.at[core,x,y,i],g.at[core,x,y,i],sd.at[d],qd.at[i],by_z(d)).wait_send()
    lo=pl.ds(0,3); hi=pl.ds(3,3)
    part=lambda a,b,h: g.at[core,a,b,h]
    es=[send(part(x,y,lo),part(x,y,lo),se,qe,d,by_x(d)) for d in range(1,4)]
    es+=[send(part(x,y,hi),part(x,y,hi),se,qe,d+4,by_y(d)) for d in range(1,4)]
    for c in es: c.wait()
    row=lambda b: g.at[core,:,b,lo]
    column=lambda a: g.at[core,a,:,hi]
    half_row=lambda b,n: g.at[core,n:n+2,b,lo]
    half_column=lambda a,n: g.at[core,a,n:n+2,hi]
    r1=send(row(y),row(y),sf,qf,1,by_y(1)); k1=send(column(x),column(x),sf,qf,5,by_x(1))
    r3=send(row(y),row(y),sf,qf,3,by_y(3)); k3=send(column(x),column(x),sf,qf,7,by_x(3))
    gs=[send(row(y),row(y),sg,qg,0,sibling),send(column(x),column(x),sg,qg,4,sibling)]
    yp,ym,xp,xm=(y+1)%4,(y+3)%4,(x+1)%4,(x+3)%4
    r1.wait_recv(); r2=send(half_row(ym,0),half_row(ym,0),sf,qf,2,by_y(1))
    k1.wait_recv(); k2=send(half_column(xm,0),half_column(xm,0),sf,qf,6,by_x(1))
    r3.wait_recv(); r0=send(half_row(yp,2),half_row(yp,2),sf,qf,0,by_y(3))
    k3.wait_recv(); k0=send(half_column(xp,2),half_column(xp,2),sf,qf,4,by_x(3))
    gs+=[send(row(ym),row(ym),sg,qg,1,sibling),send(column(xm),column(xm),sg,qg,5,sibling)]
    gs+=[send(row(yp),row(yp),sg,qg,3,sibling),send(column(xp),column(xp),sg,qg,7,sibling)]
    r2.wait_recv(); r0.wait_recv()
    gs.append(send(row((y+2)%4),row((y+2)%4),sg,qg,2,sibling))
    k2.wait_recv(); k0.wait_recv()
    gs.append(send(column((x+2)%4),column((x+2)%4),sg,qg,6,sibling))
    for c in (r0,r1,r2,r3,k0,k1,k2,k3): c.wait_send()
    for c in ms: c.wait()
    for c in gs: c.wait()
    def assemble(i,carry):
        a=i//4; b=i%4
        for o in range(2):
            for n,q in enumerate(SEEN):
                for u in range(2):
                    c0=((q%2)*2+o)*2*TILE
                    out[pl.ds(pl.multiple_of((q//2*2+u)*TILE+i*8,8),8),c0:c0+2*TILE]=g[o,a,b,n,u]
        return carry
    lax.fori_loop(0,16,assemble,0)

def total(cross,flags,parent_diag,meta):
    f32=lambda *s: pltpu.VMEM(s,jnp.float32)
    sem=lambda n: pltpu.SemaphoreType.DMA((n,))
    return pl.pallas_call(total_kernel,
        out_shape=(jax.ShapeDtypeStruct((W,W),jnp.float32),jax.ShapeDtypeStruct((4,4,4,8,TILE),jnp.int32)),
        in_specs=[VM]*4,out_specs=(VM,VM),
        scratch_shapes=[f32(4,TILE+8,TILE),f32(4,TILE+8,TILE),f32(2,TILE,2*TILE),f32(4,2,32,2*TILE),f32(2,32,2*TILE),f32(4,2,8,2*TILE),
          f32(2,4,4,6,2,8,2*TILE)]+[sem(4)]*6+[sem(8)]*8+[sem(12)]*2,
        compiler_params=pltpu.CompilerParams(collective_id=1,has_side_effects=True,vmem_limit_bytes=32*2**20),name="total",
        cost_estimate=pl.CostEstimate(flops=0,bytes_accessed=2**26,transcendentals=0))(cross,flags,parent_diag,meta)

def factor_kernel(own_ref,whole_ref,rows_ref,xh_ref,xl_ref,ih_ref,il_ref,m,x,e,sems,*rest):
    n=rows_ref.shape[0]; h=own_ref.shape[0]; blocks=W//h
    me=lax.axis_index("blk")
    cp=[pltpu.make_async_copy(own_ref,m.at[pl.ds(pl.multiple_of(me*h,h),h),:],sems.at[0])]
    for d in range(1,blocks):
        r=pl.ds(pl.multiple_of(lax.rem(me+d,blocks)*h,h),h)
        cp.append(pltpu.make_async_copy(whole_ref.at[r,:],m.at[r,:],sems.at[d]))
    cp.append(pltpu.make_async_copy(rows_ref,x,sems.at[blocks]))
    for c in cp: c.start()
    for c in cp: c.wait()
    chol_solve(m,x,n,e,*rest)
    for i in range(n//TILE):
        r=slice(i*TILE,(i+1)*TILE)
        a,b=split(x[r,:]); xh_ref[r,:]=a; xl_ref[r,:]=b
    for i in range(W//TILE):
        r=slice(i*TILE,(i+1)*TILE)
        a,b=split(e[r,:]); ih_ref[r,:]=a; il_ref[r,:]=b

def factor_child(own,whole,rows):
    n=rows.shape[0]
    b=lambda r: jax.ShapeDtypeStruct((r,W),jnp.bfloat16)
    return pl.pallas_call(factor_kernel,out_shape=(b(n),b(n),b(W),b(W)),in_specs=[HBM]*3,out_specs=(VM,)*4,
        scratch_shapes=[pltpu.VMEM((W,W),jnp.float32),pltpu.VMEM((n,W),jnp.float32),pltpu.VMEM((W,W),jnp.float32),
          pltpu.SemaphoreType.DMA((8,))]+scratch(),
        compiler_params=pltpu.CompilerParams(vmem_limit_bytes=56*2**20),name="factor_child",
        cost_estimate=pl.CostEstimate(flops=2**36,bytes_accessed=2**24,transcendentals=0))(own,whole,rows)

def dot3n(ah,al,bh,bl):
    f=lambda p,q: jnp.dot(p,q,preferred_element_type=jnp.float32)
    return f(ah,bh)+(f(ah,bl)+f(al,bh))

def schur_kernel(*refs):
    operands,(schur_ref,cross_ref,t,th,tl),loaded,sems=refs[:5],refs[5:10],refs[10:15],refs[15]
    copies=[pltpu.make_async_copy(a,b,sems.at[i]) for i,(a,b) in enumerate(zip(operands,loaded))]
    for c in copies: c.start()
    top_ref,xh,xl,ih,il=loaded
    T=top_ref.shape[0]; n=xh.shape[0]
    for i in (0,3,4): copies[i].wait()
    for r in pieces(0,T):
        a,b=split(top_ref[r,:])
        y=dot3n(a,b,ih[...],il[...])
        t[r,:]=y
        a,b=split(y); th[r,:]=a; tl[r,:]=b
    me=lax.axis_index("blk")
    cross_ref[...]=dot_nt(t[pl.ds(pl.multiple_of(me*TILE,TILE),TILE),:],t[...])
    for i in (1,2): copies[i].wait()
    for r in pieces(0,n):
        y=dot3(xh[r,:],xl[r,:],th[...],tl[...])
        for q in range(T//TILE):
            schur_ref[q,r,:]=y[:,q*TILE:(q+1)*TILE]

def schur_tiles(top,xh,xl,ih,il):
    T=top.shape[0]; n=xh.shape[0]
    return pl.pallas_call(schur_kernel,
        out_shape=(jax.ShapeDtypeStruct((T//TILE,n,TILE),jnp.float32),jax.ShapeDtypeStruct((TILE,T),jnp.float32)),
        in_specs=[HBM]*5,out_specs=(VM,VM),
        scratch_shapes=[pltpu.VMEM((T,W),jnp.float32),pltpu.VMEM((T,W),jnp.bfloat16),pltpu.VMEM((T,W),jnp.bfloat16)]
          +[pltpu.VMEM(v.shape,v.dtype) for v in (top,xh,xl,ih,il)]+[pltpu.SemaphoreType.DMA((5,))],
        compiler_params=pltpu.CompilerParams(vmem_limit_bytes=56*2**20),name="schur_tiles",
        cost_estimate=pl.CostEstimate(flops=2**33,bytes_accessed=2**24,transcendentals=0))(top,xh,xl,ih,il)

def parent(a):
    return pl.pallas_call(parent_kernel,
        out_shape=(jax.ShapeDtypeStruct((W,W),jnp.float32),)*2,
        in_specs=[HBM],out_specs=(VM,VM),
        scratch_shapes=[pltpu.VMEM((W,W),jnp.float32),pltpu.SemaphoreType.DMA]+scratch(),
        compiler_params=pltpu.CompilerParams(vmem_limit_bytes=56*2**20),name="parent",
        cost_estimate=pl.CostEstimate(flops=6*2**30,bytes_accessed=2**24,transcendentals=0))(a)

def place_kernel(position,tiles,out,sems):
    copies=[pltpu.make_async_copy(tiles.at[i],out.at[position[i]],sems.at[i]) for i in range(tiles.shape[0])]
    for c in copies: c.start()
    for c in copies: c.wait()

def place(position,tiles,slots):
    return pl.pallas_call(place_kernel,
        out_shape=jax.ShapeDtypeStruct((slots,TILE,TILE),jnp.float32),
        in_specs=[pl.BlockSpec(memory_space=pltpu.SMEM),VM],out_specs=HBM,
        scratch_shapes=[pltpu.SemaphoreType.DMA((tiles.shape[0],))],name="place")(position,tiles)

def subtract_kernel(labels,received,rows,out,held,sems):
    count=sems.shape[0]; each=held.shape[0]//count
    copies=[pltpu.make_async_copy(received.at[i*each:(i+1)*each],held.at[i*each:(i+1)*each],sems.at[i]) for i in range(count)]
    for c in copies: c.start()
    for p in range(PB):
        out[p]=rows[p*TILE:(p+1)*TILE,:]
    def one(i,carry):
        label=labels[i]
        @pl.when(label>=0)
        def _():
            slot=label//2
            columns=pl.ds(pl.multiple_of((label-slot*2)*TILE,TILE),TILE)
            out[slot,:,columns]=out[slot,:,columns]-held[i]
        return carry
    for i,c in enumerate(copies):
        c.wait()
        lax.fori_loop(i*each,(i+1)*each,one,0)

def subtract(labels,received,rows):
    width=rows.shape[1]
    return pl.pallas_call(subtract_kernel,
        out_shape=jax.ShapeDtypeStruct((PB,TILE,width),jnp.float32),
        in_specs=[pl.BlockSpec(memory_space=pltpu.SMEM),HBM,VM],out_specs=VM,
        scratch_shapes=[pltpu.VMEM(received.shape,jnp.float32),pltpu.SemaphoreType.DMA((8,))],
        compiler_params=pltpu.CompilerParams(vmem_limit_bytes=40*2**20),name="subtract")(labels,received,rows)

def shards(child_diag,child_top,child_rows,row_owner,row_slot,col_block,parent_diag,parent_rows):
    blocks=lax.axis_size("blk"); fronts=lax.axis_size("front")
    my_block=lax.axis_index("blk")
    quarter=W//(TILE*blocks)
    capacity=2
    owners=row_owner[0,:,0]
    column_picks=col_block[0]
    block_ids=jnp.arange(blocks,dtype=jnp.int32)
    my_pick=jnp.sum(jnp.where(block_ids==my_block,column_picks,0))
    sequence=jnp.arange(owners.shape[0],dtype=jnp.int32)
    earlier=(owners[:,None]==owners[None,:])&(sequence[None,:]<sequence[:,None])
    position=owners*capacity+jnp.sum(earlier.astype(jnp.int32),axis=1)
    diag_whole=gather(child_diag,blocks)
    my_top,diag_whole=lax.optimization_barrier((child_top,diag_whole))
    top_whole=lax.all_gather(my_top,"blk",axis=0,tiled=True)
    schur,cross=schur_tiles(top_whole,*factor_child(child_diag,diag_whole,child_rows))
    pairs=jnp.arange(8,dtype=jnp.int32)
    flags=(pairs[None,:]//2==my_pick)&(pairs[None,:]%2==column_picks[:,None])&(pairs[None,:]<4)
    flags=jnp.broadcast_to(flags.astype(jnp.float32)[:,:,None],(blocks,8,TILE))
    meta=jnp.zeros((8,TILE),jnp.int32).at[0,0:owners.shape[0]].set(owners).at[1,0:owners.shape[0]].set(row_slot[0])
    meta=meta.at[2,0:blocks].set(column_picks)
    whole,everyone=total(cross,flags,parent_diag,meta)
    arrived=lax.all_to_all(schur,"blk",split_axis=0,concat_axis=0,tiled=True).reshape(blocks*TA,TILE,TILE)
    arrived,whole,everyone=lax.optimization_barrier((arrived,whole,everyone))
    outgoing=place(position,arrived,fronts*capacity)
    received=lax.all_to_all(outgoing.reshape(fronts,capacity,TILE,TILE),"front",split_axis=0,concat_axis=0,tiled=True)
    everyone=everyone.reshape(fronts,8,TILE)
    all_owners=everyone[:,0,0:owners.shape[0]]
    ours=all_owners==lax.axis_index("front")
    nth=jnp.sum((ours[:,None,:]&(sequence[None,None,:]<sequence[None,:,None])).astype(jnp.int32),axis=2)
    their_pick=jnp.sum(jnp.where(block_ids==my_block,everyone[:,2,0:blocks],0),axis=1)
    landing=everyone[:,1,0:owners.shape[0]]*quarter+their_pick[:,None]
    turn=jnp.arange(capacity,dtype=jnp.int32)
    labels=jnp.max(jnp.where(ours[:,None,:]&(nth[:,None,:]==turn[None,:,None]),landing[:,None,:],-1),axis=2).reshape(-1)
    factor,inverse=parent(whole)
    received,inverse,factor=lax.optimization_barrier((received,inverse,factor))
    updated=subtract(labels,received.reshape(-1,TILE,TILE),parent_rows)
    row_major=lax.all_to_all(updated,"blk",split_axis=0,concat_axis=2,tiled=True)
    row_major=row_major.reshape(TILE,W)
    height=parent_diag.shape[0]
    own=lax.dynamic_slice_in_dim(factor,my_block*height,height,0)
    panel=jnp.dot(row_major,inverse,precision=HIGHEST)
    return own,panel


def solution(mesh):
    return jax.shard_map(shards,mesh=mesh,
        in_specs=(P(("front","blk"),None),P(("front","blk"),None),P(("front","blk"),None),P("front",None,None),
                  P("front",None),P("front",None),P("blk",None),P("front","blk")),
        out_specs=(P("blk",None),P(("front","blk"),None)),check_vma=False)
```

```python
import functools
import jax
import jax.numpy as jnp
from jax import lax
from jax.experimental import pallas as pl
from jax.experimental.pallas import tpu as pltpu
from jax.sharding import PartitionSpec as P

W = 1024
TILE = 128
TA = 4
PB = 4
SUB = 8
HIGHEST=lax.Precision.HIGHEST
NT=(((1,),(1,)),((),()))

def dot_nt(a,b):
    return lax.dot_general(a,b,NT,precision=HIGHEST,preferred_element_type=jnp.float32)

def split(x):
    hi=x.astype(jnp.bfloat16)
    lo=(x-hi.astype(jnp.float32)).astype(jnp.bfloat16)
    return hi,lo

def dot3(ah,al,bh,bl):
    f=lambda p,q: lax.dot_general(p,q,NT,preferred_element_type=jnp.float32)
    return f(ah,bh)+(f(ah,bl)+f(al,bh))

def recip(x):
    return pltpu.reciprocal(x,approx=True)

def diag_steps(s):
    lane=lax.broadcasted_iota(jnp.int32,(SUB,TILE),1)
    sub=lax.broadcasted_iota(jnp.int32,(SUB,TILE),0)
    full=(SUB,TILE)
    following=s[0:SUB,:]
    for b in range(TILE//SUB):
        r0=b*SUB
        inside=(lane>=r0)&(lane<r0+SUB)
        v=[jnp.broadcast_to(following[i:i+1,:],full) for i in range(SUB)]
        a=[[jnp.broadcast_to(v[i][:,r0+j:r0+j+1],full) for j in range(i+1)] for i in range(SUB)]
        w=[jnp.where(inside,jnp.where(lane==r0+i,1.0,0.0),v[i]) for i in range(SUB)]
        r=[None]*SUB
        l=[[None]*SUB for _ in range(SUB)]
        for i in range(SUB):
            r[i]=recip(a[i][i])
            for k in range(i+1,SUB):
                l[k][i]=a[k][i]*r[i]
            for k in range(i+1,SUB):
                for m in range(i+1,k+1):
                    a[k][m]=a[k][m]-l[k][i]*a[m][i]
            for k in range(i+1,SUB):
                w[k]=w[k]-l[k][i]*w[i]
        z=[w[i]*r[i] for i in range(SUB)]
        for i in range(SUB-1,0,-1):
            for k in range(i):
                z[k]=z[k]-l[i][k]*z[i]
        far=(b+2)*SUB
        if far<TILE:
            whole=z[0]
            for i in range(1,SUB): whole=jnp.where(sub==i,z[i],whole)
            x=s[far:,:]
            y=jnp.dot(x[:,r0:r0+SUB],whole,precision=HIGHEST,preferred_element_type=jnp.float32)
            rest=jnp.where(lax.broadcasted_iota(jnp.int32,x.shape,1)//SUB==b,0.0,x)-y
        if b+1<TILE//SUB:
            x=s[r0+SUB:far,:]
            c=[jnp.broadcast_to(x[:,r0+i:r0+i+1],full) for i in range(SUB)]
            p=c[0]*z[0]
            q=c[1]*z[1]
            for i in range(2,SUB,2):
                p=p+c[i]*z[i]
                q=q+c[i+1]*z[i+1]
            following=jnp.where(inside,0.0,x)-(p+q)
        if far<TILE:
            s[far:,:]=rest
        o=w[0]*lax.rsqrt(a[0][0])
        for i in range(1,SUB):
            o=jnp.where(sub==i,w[i]*lax.rsqrt(a[i][i]),o)
        s[r0:r0+SUB,:]=jnp.where(lane<r0+SUB,o,0.0)
        yield b

def diag(s):
    for _ in diag_steps(s): pass


def block(start,size=TILE):
    return pl.ds(pl.multiple_of(start,TILE),size)

def pieces(start,stop,size=256):
    return [slice(r,min(r+size,stop)) for r in range(start,stop,size)]

def chol_solve(m,x,n,e,s,inv_hi,inv_lo,p_hi,p_lo,low=None):
    s[...]=m[0:TILE,0:TILE]
    if low is not None:
        low[...]=jnp.zeros((W,W),jnp.float32)
        low[0:TILE,0:TILE]=m[0:TILE,0:TILE]
    e[...]=jnp.zeros((W,W),jnp.float32)
    diag(s)
    steps=TILE//SUB
    for c0 in range(0,W,TILE):
        c1=c0+TILE
        inv=s[...]
        ih,il=split(inv)
        inv_hi[...]=ih; inv_lo[...]=il
        if low is not None:
            low[c0:c1,c0:c1]=dot_nt(low[c0:c1,c0:c1],inv)
        e[c0:c1,c0:c1]=inv.T
        if c1<W:
            p=dot_nt(m[c1:c1+TILE,c0:c1],inv)
            new=m[c1:c1+TILE,c1:c1+TILE]-dot_nt(p,p)
            s[...]=new
            if low is not None:
                low[c1:c1+TILE,c1:c1+TILE]=new
        def solved(ref,r):
            a,b=split(ref[r,c0:c1])
            q=dot3(a,b,inv_hi[...],inv_lo[...])
            return q,split(q)
        def panel(r):
            q,(a,b)=solved(m,r)
            p_hi[r,:]=a; p_lo[r,:]=b
            if low is not None:
                low[r,c0:c1]=q
        def trail(r):
            end=r.stop
            m[r,c1:end]=m[r,c1:end]-dot3(p_hi[r,:],p_lo[r,:],p_hi[c1:end,:],p_lo[c1:end,:])
        def other(ref,r):
            q,(a,b)=solved(ref,r)
            if c1<W:
                ref[r,c1:]=ref[r,c1:]-dot3(a,b,p_hi[c1:,:],p_lo[c1:,:])
            ref[r,c0:c1]=q
        def start(r):
            e[r,c1:]=-dot3(*split(e[r,c0:c1]),p_hi[c1:,:],p_lo[c1:,:])
        work=[functools.partial(panel,r) for r in pieces(c1,W)]
        work+=[functools.partial(trail,r) for r in pieces(c1,W)]
        work+=[functools.partial(other,x,r) for r in pieces(0,n)]
        work+=[functools.partial(other,e,r) for r in pieces(0,c0)]
        if c1<W:
            work+=[functools.partial(start,slice(c0,c1))]
            done=0
            for b in diag_steps(s):
                upto=(b+1)*len(work)//steps
                for f in work[done:upto]: f()
                done=upto
        else:
            for f in work: f()

def scratch():
    b=jnp.bfloat16
    return [pltpu.VMEM((TILE,TILE),jnp.float32),pltpu.VMEM((TILE,TILE),b),pltpu.VMEM((TILE,TILE),b),
            pltpu.VMEM((W,TILE),b),pltpu.VMEM((W,TILE),b)]

HBM=pl.BlockSpec(memory_space=pl.ANY)
VM=pl.BlockSpec(memory_space=pltpu.VMEM)

def parent_kernel(a_ref,low_ref,ih_ref,il_ref,m,e,sem,*rest):
    c=pltpu.make_async_copy(a_ref,m,sem); c.start(); c.wait()
    chol_solve(m,None,0,e,*rest,low=low_ref)
    for r in pieces(0,W):
        a,b=split(e[r,:]); ih_ref[r,:]=a; il_ref[r,:]=b

MESH = pl.DeviceIdType.MESH

def greet(partners):
    barrier=pltpu.get_barrier_semaphore()
    for p in partners:
        pl.semaphore_signal(barrier,inc=1,device_id=p,device_id_type=MESH)
    pl.semaphore_wait(barrier,len(partners))

PIECES = (
    ((0,0,1,1),(1,0,2,1)),
    ((0,0,3,-1),(1,0,4,-1)),
    ((0,2,5,-1),(1,0,3,-1),(1,3,6,-1),(0,0,2,1)),
    ((0,4,7,1),(1,0,4,1),(1,4,8,1),(0,0,4,-1)),
)

def gather_kernel(blocks,mine,whole,send,recv,pass_sem):
    front=lax.axis_index("front"); me=lax.axis_index("blk")
    to=lambda d: (front,lax.rem(me+d+blocks,blocks))
    greet([to(d) for d in range(1,blocks)])
    h=mine.shape[0]; half=h//2
    def move(k,i,d,first):
        part,a,b,_=PIECES[k][i]
        rows=slice(part*half,(part+1)*half); columns=slice(a*TILE,b*TILE)
        there=whole.at[k*h+part*half:k*h+(part+1)*half,columns]
        sem=send.at[i,(d+1)//2] if first else pass_sem.at[k,i]
        return pltpu.make_async_remote_copy(src_ref=mine.at[rows,columns] if first else there,dst_ref=there,
            send_sem=sem,recv_sem=recv.at[k,i],device_id=to(d),device_id_type=MESH)
    def order(k,d):
        count=range(len(PIECES[k]))
        return [i for i in count if PIECES[k][i][3]==d]+[i for i in count if PIECES[k][i][3]!=d]
    for k in range(blocks):
        @pl.when(me==k)
        def _():
            for a,b in zip(order(k,1),order(k,-1)):
                move(k,a,1,True).start(); move(k,b,-1,True).start()
    for i in range(4):
        for k in range(blocks):
            for d in (1,-1):
                if i<len(PIECES[k]) and PIECES[k][i][3]==d:
                    @pl.when(me==(k+d)%blocks)
                    def _():
                        c=move(k,i,d,False); c.wait_recv(); c.start()
    for k in range(blocks):
        for d in (1,-1):
            @pl.when(me==(k+d)%blocks)
            def _():
                for i in range(len(PIECES[k])):
                    if PIECES[k][i][3]==d: move(k,i,d,False).wait_send()
                    else: move(k,i,d,False).wait_recv()
        @pl.when(me==(k+2)%blocks)
        def _():
            for i in range(len(PIECES[k])): move(k,i,1,False).wait_recv()
        @pl.when(me==k)
        def _():
            for i in range(len(PIECES[k])):
                for d in (1,-1): move(k,i,d,True).wait_send()

def gather(mine,blocks):
    h=mine.shape[0]
    return pl.pallas_call(functools.partial(gather_kernel,blocks),
        out_shape=jax.ShapeDtypeStruct((h*blocks,W),jnp.float32),in_specs=[HBM],out_specs=HBM,
        scratch_shapes=[pltpu.SemaphoreType.DMA((4,2)),pltpu.SemaphoreType.DMA((blocks,4)),pltpu.SemaphoreType.DMA((blocks,4))],
        compiler_params=pltpu.CompilerParams(collective_id=0,has_side_effects=True),name="gather_diag",
        cost_estimate=pl.CostEstimate(flops=0,bytes_accessed=2**23,transcendentals=0))(mine)

SEEN = (0, 2, 4, 5, 6, 7)

def total_kernel(cross,flags,pd,meta,out,everyone,msg,ra,a1,rb,a2,rc,g,sa,qa,sb,qb,sc,qc,sd,qd,se,qe,sf,qf,sg,qg,sm,qm):
    front=lax.axis_index("front"); k=lax.axis_index("blk")
    x=front//16; y=(front//4)%4; zl=(front//2)%2; core=front%2
    l=zl*2+core; pos=k*2+zl
    at=lambda x,y,l: (x*16+y*4+l)
    def by_l(d): return (at(x,y,(l+d)%4),k)
    def by_x(d): return (at((x+d)%4,y,l),k)
    def by_y(d): return (at(x,(y+d)%4,l),k)
    def by_z(d):
        q=(pos+d)%8
        return (at(x,y,(q%2)*2+core),q//2)
    sibling=(at(x,y,zl*2+1-core),k)
    greet([by_l(d) for d in range(1,4)]+[by_x(d) for d in range(1,4)]+[by_y(d) for d in range(1,4)]+[by_z(d) for d in range(1,8)]+[sibling])
    def describe(src,dst,s,q,who):
        return pltpu.make_async_remote_copy(src_ref=src,dst_ref=dst,send_sem=s,recv_sem=q,device_id=who,device_id_type=MESH)
    def send(src,dst,s,q,i,who):
        c=describe(src,dst,s.at[i],q.at[i],who)
        c.start()
        return c
    for i in range(4):
        msg[i,0:TILE,:]=cross[:,i*TILE:(i+1)*TILE]
        msg[i,TILE:TILE+8,:]=flags[i]
    everyone[x,y,l]=meta[...]
    cs=[send(msg.at[(l+d)%4],ra.at[d],sa,qa,d,by_l(d)) for d in range(1,4)]
    cs+=[send(everyone.at[x,y,l],everyone.at[x,y,l],sm,qm,d,by_l(d)) for d in range(1,4)]
    ra[0]=msg[l]
    for c in cs: c.wait()
    for u in range(2):
        for v in range(2):
            t=None
            for i in range(4):
                p=ra[i,0:TILE,:]*ra[i,TILE+2*u+v:TILE+2*u+v+1,:]
                t=p if t is None else t+p
            a1[u,:,v*TILE:(v+1)*TILE]=t
    rows=lambda q,n: pl.ds(pl.multiple_of(q*n,n),n)
    cs=[send(a1.at[:,rows((x+d)%4,32),:],rb.at[d],sb,qb,d,by_x(d)) for d in range(1,4)]
    cs+=[send(everyone.at[x,y],everyone.at[x,y],sm,qm,d+4,by_x(d)) for d in range(1,4)]
    rb[0]=a1[:,rows(x,32),:]
    for c in cs: c.wait()
    a2[...]=(rb[0]+rb[1])+(rb[2]+rb[3])
    cs=[send(a2.at[:,rows((y+d)%4,8),:],rc.at[d],sc,qc,d,by_y(d)) for d in range(1,4)]
    ms=[send(everyone.at[:,y],everyone.at[:,y],sm,qm,d+8,by_y(d)) for d in range(1,4)]
    rc[0]=a2[:,rows(y,8),:]
    for c in cs: c.wait()
    t=(rc[0]+rc[1])+(rc[2]+rc[3])
    for i,q in enumerate(SEEN):
        @pl.when(pos==q)
        def _():
            for u in range(2):
                g[core,x,y,i,u]=pd[pl.ds(pl.multiple_of(u*TILE+(x*4+y)*8,8),8),pl.ds(pl.multiple_of(l*2*TILE,TILE),2*TILE)]-t[u]
            for d in range(1,8):
                describe(g.at[core,x,y,i],g.at[core,x,y,i],sd.at[d],qd.at[i],by_z(d)).start()
    for i,q in enumerate(SEEN):
        @pl.when(pos!=q)
        def _():
            describe(g.at[core,x,y,i],g.at[core,x,y,i],sd.at[0],qd.at[i],by_z(1)).wait_recv()
    for i,q in enumerate(SEEN):
        @pl.when(pos==q)
        def _():
            for d in range(1,8):
                describe(g.at[core,x,y,i],g.at[core,x,y,i],sd.at[d],qd.at[i],by_z(d)).wait_send()
    lo=pl.ds(0,3); hi=pl.ds(3,3)
    part=lambda a,b,h: g.at[core,a,b,h]
    es=[send(part(x,y,lo),part(x,y,lo),se,qe,d,by_x(d)) for d in range(1,4)]
    es+=[send(part(x,y,hi),part(x,y,hi),se,qe,d+4,by_y(d)) for d in range(1,4)]
    for c in es: c.wait()
    row=lambda b: g.at[core,:,b,lo]
    column=lambda a: g.at[core,a,:,hi]
    half_row=lambda b,n: g.at[core,n:n+2,b,lo]
    half_column=lambda a,n: g.at[core,a,n:n+2,hi]
    r1=send(row(y),row(y),sf,qf,1,by_y(1)); k1=send(column(x),column(x),sf,qf,5,by_x(1))
    r3=send(row(y),row(y),sf,qf,3,by_y(3)); k3=send(column(x),column(x),sf,qf,7,by_x(3))
    gs=[send(row(y),row(y),sg,qg,0,sibling),send(column(x),column(x),sg,qg,4,sibling)]
    yp,ym,xp,xm=(y+1)%4,(y+3)%4,(x+1)%4,(x+3)%4
    r1.wait_recv(); r2=send(half_row(ym,0),half_row(ym,0),sf,qf,2,by_y(1))
    k1.wait_recv(); k2=send(half_column(xm,0),half_column(xm,0),sf,qf,6,by_x(1))
    r3.wait_recv(); r0=send(half_row(yp,2),half_row(yp,2),sf,qf,0,by_y(3))
    k3.wait_recv(); k0=send(half_column(xp,2),half_column(xp,2),sf,qf,4,by_x(3))
    gs+=[send(row(ym),row(ym),sg,qg,1,sibling),send(column(xm),column(xm),sg,qg,5,sibling)]
    gs+=[send(row(yp),row(yp),sg,qg,3,sibling),send(column(xp),column(xp),sg,qg,7,sibling)]
    r2.wait_recv(); r0.wait_recv()
    gs.append(send(row((y+2)%4),row((y+2)%4),sg,qg,2,sibling))
    k2.wait_recv(); k0.wait_recv()
    gs.append(send(column((x+2)%4),column((x+2)%4),sg,qg,6,sibling))
    for c in (r0,r1,r2,r3,k0,k1,k2,k3): c.wait_send()
    for c in ms: c.wait()
    for c in gs: c.wait()
    def assemble(i,carry):
        a=i//4; b=i%4
        for o in range(2):
            for n,q in enumerate(SEEN):
                for u in range(2):
                    c0=((q%2)*2+o)*2*TILE
                    out[pl.ds(pl.multiple_of((q//2*2+u)*TILE+i*8,8),8),c0:c0+2*TILE]=g[o,a,b,n,u]
        return carry
    lax.fori_loop(0,16,assemble,0)

def total(cross,flags,parent_diag,meta):
    f32=lambda *s: pltpu.VMEM(s,jnp.float32)
    sem=lambda n: pltpu.SemaphoreType.DMA((n,))
    return pl.pallas_call(total_kernel,
        out_shape=(jax.ShapeDtypeStruct((W,W),jnp.float32),jax.ShapeDtypeStruct((4,4,4,8,TILE),jnp.int32)),
        in_specs=[VM]*4,out_specs=(VM,VM),
        scratch_shapes=[f32(4,TILE+8,TILE),f32(4,TILE+8,TILE),f32(2,TILE,2*TILE),f32(4,2,32,2*TILE),f32(2,32,2*TILE),f32(4,2,8,2*TILE),
          f32(2,4,4,6,2,8,2*TILE)]+[sem(4)]*6+[sem(8)]*8+[sem(12)]*2,
        compiler_params=pltpu.CompilerParams(collective_id=1,has_side_effects=True,vmem_limit_bytes=32*2**20),name="total",
        cost_estimate=pl.CostEstimate(flops=0,bytes_accessed=2**26,transcendentals=0))(cross,flags,parent_diag,meta)

def factor_kernel(own_ref,whole_ref,rows_ref,xh_ref,xl_ref,ih_ref,il_ref,m,x,e,sems,*rest):
    n=rows_ref.shape[0]; h=own_ref.shape[0]; blocks=W//h
    me=lax.axis_index("blk")
    cp=[pltpu.make_async_copy(own_ref,m.at[pl.ds(pl.multiple_of(me*h,h),h),:],sems.at[0])]
    for d in range(1,blocks):
        r=pl.ds(pl.multiple_of(lax.rem(me+d,blocks)*h,h),h)
        cp.append(pltpu.make_async_copy(whole_ref.at[r,:],m.at[r,:],sems.at[d]))
    cp.append(pltpu.make_async_copy(rows_ref,x,sems.at[blocks]))
    for c in cp: c.start()
    for c in cp: c.wait()
    chol_solve(m,x,n,e,*rest)
    for i in range(n//TILE):
        r=slice(i*TILE,(i+1)*TILE)
        a,b=split(x[r,:]); xh_ref[r,:]=a; xl_ref[r,:]=b
    for i in range(W//TILE):
        r=slice(i*TILE,(i+1)*TILE)
        a,b=split(e[r,:]); ih_ref[r,:]=a; il_ref[r,:]=b

def factor_child(own,whole,rows):
    n=rows.shape[0]
    b=lambda r: jax.ShapeDtypeStruct((r,W),jnp.bfloat16)
    return pl.pallas_call(factor_kernel,out_shape=(b(n),b(n),b(W),b(W)),in_specs=[HBM]*3,out_specs=(VM,)*4,
        scratch_shapes=[pltpu.VMEM((W,W),jnp.float32),pltpu.VMEM((n,W),jnp.float32),pltpu.VMEM((W,W),jnp.float32),
          pltpu.SemaphoreType.DMA((8,))]+scratch(),
        compiler_params=pltpu.CompilerParams(vmem_limit_bytes=56*2**20),name="factor_child",
        cost_estimate=pl.CostEstimate(flops=2**36,bytes_accessed=2**24,transcendentals=0))(own,whole,rows)

def dot3n(ah,al,bh,bl):
    f=lambda p,q: jnp.dot(p,q,preferred_element_type=jnp.float32)
    return f(ah,bh)+(f(ah,bl)+f(al,bh))

def schur_kernel(*refs):
    operands,(schur_ref,cross_ref,t,th,tl),loaded,sems=refs[:5],refs[5:10],refs[10:15],refs[15]
    copies=[pltpu.make_async_copy(a,b,sems.at[i]) for i,(a,b) in enumerate(zip(operands,loaded))]
    for c in copies: c.start()
    top_ref,xh,xl,ih,il=loaded
    T=top_ref.shape[0]; n=xh.shape[0]
    for i in (0,3,4): copies[i].wait()
    for r in pieces(0,T):
        a,b=split(top_ref[r,:])
        y=dot3n(a,b,ih[...],il[...])
        t[r,:]=y
        a,b=split(y); th[r,:]=a; tl[r,:]=b
    me=lax.axis_index("blk")
    cross_ref[...]=dot_nt(t[pl.ds(pl.multiple_of(me*TILE,TILE),TILE),:],t[...])
    for i in (1,2): copies[i].wait()
    for r in pieces(0,n):
        y=dot3(xh[r,:],xl[r,:],th[...],tl[...])
        for q in range(T//TILE):
            schur_ref[q,r,:]=y[:,q*TILE:(q+1)*TILE]

def schur_tiles(top,xh,xl,ih,il):
    T=top.shape[0]; n=xh.shape[0]
    return pl.pallas_call(schur_kernel,
        out_shape=(jax.ShapeDtypeStruct((T//TILE,n,TILE),jnp.float32),jax.ShapeDtypeStruct((TILE,T),jnp.float32)),
        in_specs=[HBM]*5,out_specs=(VM,VM),
        scratch_shapes=[pltpu.VMEM((T,W),jnp.float32),pltpu.VMEM((T,W),jnp.bfloat16),pltpu.VMEM((T,W),jnp.bfloat16)]
          +[pltpu.VMEM(v.shape,v.dtype) for v in (top,xh,xl,ih,il)]+[pltpu.SemaphoreType.DMA((5,))],
        compiler_params=pltpu.CompilerParams(vmem_limit_bytes=56*2**20),name="schur_tiles",
        cost_estimate=pl.CostEstimate(flops=2**33,bytes_accessed=2**24,transcendentals=0))(top,xh,xl,ih,il)

def parent(a):
    return pl.pallas_call(parent_kernel,
        out_shape=(jax.ShapeDtypeStruct((W,W),jnp.float32),)+(jax.ShapeDtypeStruct((W,W),jnp.bfloat16),)*2,
        in_specs=[HBM],out_specs=(VM,)*3,
        scratch_shapes=[pltpu.VMEM((W,W),jnp.float32),pltpu.VMEM((W,W),jnp.float32),pltpu.SemaphoreType.DMA]+scratch(),
        compiler_params=pltpu.CompilerParams(vmem_limit_bytes=56*2**20),name="parent",
        cost_estimate=pl.CostEstimate(flops=6*2**30,bytes_accessed=2**24,transcendentals=0))(a)

def place_kernel(position,tiles,out,sems):
    copies=[pltpu.make_async_copy(tiles.at[i],out.at[position[i]],sems.at[i]) for i in range(tiles.shape[0])]
    for c in copies: c.start()
    for c in copies: c.wait()

def place(position,tiles,slots):
    return pl.pallas_call(place_kernel,
        out_shape=jax.ShapeDtypeStruct((slots,TILE,TILE),jnp.float32),
        in_specs=[pl.BlockSpec(memory_space=pltpu.SMEM),VM],out_specs=HBM,
        scratch_shapes=[pltpu.SemaphoreType.DMA((tiles.shape[0],))],name="place")(position,tiles)

def subtract_kernel(labels,received,rows,out,held,sems):
    count=sems.shape[0]; each=held.shape[0]//count
    copies=[pltpu.make_async_copy(received.at[i*each:(i+1)*each],held.at[i*each:(i+1)*each],sems.at[i]) for i in range(count)]
    for c in copies: c.start()
    for p in range(PB):
        out[p]=rows[p*TILE:(p+1)*TILE,:]
    def one(i,carry):
        label=labels[i]
        @pl.when(label>=0)
        def _():
            slot=label//2
            columns=pl.ds(pl.multiple_of((label-slot*2)*TILE,TILE),TILE)
            out[slot,:,columns]=out[slot,:,columns]-held[i]
        return carry
    for i,c in enumerate(copies):
        c.wait()
        lax.fori_loop(i*each,(i+1)*each,one,0)

def subtract(labels,received,rows):
    width=rows.shape[1]
    return pl.pallas_call(subtract_kernel,
        out_shape=jax.ShapeDtypeStruct((PB,TILE,width),jnp.float32),
        in_specs=[pl.BlockSpec(memory_space=pltpu.SMEM),HBM,VM],out_specs=VM,
        scratch_shapes=[pltpu.VMEM(received.shape,jnp.float32),pltpu.SemaphoreType.DMA((8,))],
        compiler_params=pltpu.CompilerParams(vmem_limit_bytes=40*2**20),name="subtract")(labels,received,rows)

def finish_kernel(rows,ih,il,out):
    width=rows.shape[2]; t=None
    for q in range(rows.shape[0]):
        r=slice(q*width,(q+1)*width)
        a,b=split(rows[q])
        p=dot3n(a,b,ih[r,:],il[r,:])
        t=p if t is None else t+p
    out[...]=t

def finish(rows,ih,il):
    return pl.pallas_call(finish_kernel,out_shape=jax.ShapeDtypeStruct((rows.shape[1],W),jnp.float32),
        in_specs=[VM]*3,out_specs=VM,compiler_params=pltpu.CompilerParams(vmem_limit_bytes=16*2**20),name="finish")(rows,ih,il)

def shards(child_diag,child_top,child_rows,row_owner,row_slot,col_block,parent_diag,parent_rows):
    blocks=lax.axis_size("blk"); fronts=lax.axis_size("front")
    my_block=lax.axis_index("blk")
    quarter=W//(TILE*blocks)
    capacity=2
    owners=row_owner[0,:,0]
    column_picks=col_block[0]
    block_ids=jnp.arange(blocks,dtype=jnp.int32)
    my_pick=jnp.sum(jnp.where(block_ids==my_block,column_picks,0))
    sequence=jnp.arange(owners.shape[0],dtype=jnp.int32)
    earlier=(owners[:,None]==owners[None,:])&(sequence[None,:]<sequence[:,None])
    position=owners*capacity+jnp.sum(earlier.astype(jnp.int32),axis=1)
    diag_whole=gather(child_diag,blocks)
    my_top,diag_whole=lax.optimization_barrier((child_top,diag_whole))
    top_whole=lax.all_gather(my_top,"blk",axis=0,tiled=True)
    schur,cross=schur_tiles(top_whole,*factor_child(child_diag,diag_whole,child_rows))
    pairs=jnp.arange(8,dtype=jnp.int32)
    flags=(pairs[None,:]//2==my_pick)&(pairs[None,:]%2==column_picks[:,None])&(pairs[None,:]<4)
    flags=jnp.broadcast_to(flags.astype(jnp.float32)[:,:,None],(blocks,8,TILE))
    meta=jnp.zeros((8,TILE),jnp.int32).at[0,0:owners.shape[0]].set(owners).at[1,0:owners.shape[0]].set(row_slot[0])
    meta=meta.at[2,0:blocks].set(column_picks)
    whole,everyone=total(cross,flags,parent_diag,meta)
    arrived=lax.all_to_all(schur,"blk",split_axis=0,concat_axis=0,tiled=True).reshape(blocks*TA,TILE,TILE)
    arrived,whole,everyone=lax.optimization_barrier((arrived,whole,everyone))
    outgoing=place(position,arrived,fronts*capacity)
    received=lax.all_to_all(outgoing.reshape(fronts,capacity,TILE,TILE),"front",split_axis=0,concat_axis=0,tiled=True)
    everyone=everyone.reshape(fronts,8,TILE)
    all_owners=everyone[:,0,0:owners.shape[0]]
    ours=all_owners==lax.axis_index("front")
    nth=jnp.sum((ours[:,None,:]&(sequence[None,None,:]<sequence[None,:,None])).astype(jnp.int32),axis=2)
    their_pick=jnp.sum(jnp.where(block_ids==my_block,everyone[:,2,0:blocks],0),axis=1)
    landing=everyone[:,1,0:owners.shape[0]]*quarter+their_pick[:,None]
    turn=jnp.arange(capacity,dtype=jnp.int32)
    labels=jnp.max(jnp.where(ours[:,None,:]&(nth[:,None,:]==turn[None,:,None]),landing[:,None,:],-1),axis=2).reshape(-1)
    factor,*inverse=parent(whole)
    received,inverse,factor=lax.optimization_barrier((received,inverse,factor))
    updated=subtract(labels,received.reshape(-1,TILE,TILE),parent_rows)
    quarters=lax.all_to_all(updated,"blk",split_axis=0,concat_axis=0,tiled=True)
    height=parent_diag.shape[0]
    own=lax.dynamic_slice_in_dim(factor,my_block*height,height,0)
    panel=finish(quarters,*inverse)
    return own,panel


def solution(mesh):
    return jax.shard_map(shards,mesh=mesh,
        in_specs=(P(("front","blk"),None),P(("front","blk"),None),P(("front","blk"),None),P("front",None,None),
                  P("front",None),P("front",None),P("blk",None),P("front","blk")),
        out_specs=(P("blk",None),P(("front","blk"),None)),check_vma=False)
```
